1024 devices in a mesh: rep: 128 (over y_lo, z, core), fsdp: 8 (over x, y_hi).
Axes of the slice: x: 4, y: 4 (y_hi: 2, y_lo: 2; y = y_hi * 2 + y_lo), z: 32, core: 2. Of those that a mesh axis runs over, the one named last changes fastest.
Arguments:
- tokens: bfloat16 [131072, 4608], P('rep', 'fsdp'), may hold values from -3300 to 3300
- norm_gain: bfloat16 [128, 4608], P('rep', 'fsdp'), may hold values from 0.5 to 1.5
- key_weight: bfloat16 [128, 1024, 4608], P('rep', None, 'fsdp'), may hold values from -0.3125 to 0.3125
- key_cotangent: bfloat16 [131072, 1024], P(('rep', 'fsdp')), may hold values from -24 to 24
- global_fragment: float32 [1024, 4608], P('rep', 'fsdp'), may hold values from -6 to 6
- outer_momentum: float32 [1024, 4608], P('rep', 'fsdp'), may hold values from -3 to 3
Outputs:
- keys: bfloat16 [131072, 1024], P(('rep', 'fsdp'))
- gain_grad: float32 [128, 4608], P('rep', 'fsdp')
- new_global: float32 [1024, 4608], P('rep', 'fsdp')
- new_momentum: float32 [1024, 4608], P('rep', 'fsdp')
The draws below stay inside these ranges and needn't reach their ends.
All inputs are finite; a program needn't handle non-finite values.
Results may differ from the reference program's by a relative error of at most 0.015.
Values may be sent and summed in bfloat16 or wider, within the bound.
No kernel may reach another device: no remote copies, remote signals or barrier semaphores. Data moves between devices by JAX's collectives and lax.ppermute only.
A program may use at most 32 MiB of HBM per device.

```python
import math
import jax
import jax.numpy as jnp
from jax import lax

D = 4608
KV_COLS = 1024
TOK_REP = 1024
TOKENS = 131072
N_REP = 128
N_FSDP = 8


def draw_tokens(key, part):
    key = jax.random.fold_in(key, 17)
    key_normal, key_rows, key_cols = jax.random.split(key, 3)
    normal_part = jax.random.truncated_normal(key_normal, -4.0, 4.0, (TOKENS, D), jnp.float32)
    feature_trend = jnp.exp(jnp.arange(D, dtype=jnp.float32) * (math.log(3.0) / (D - 1)))
    row_scale = jnp.exp(jax.random.uniform(key_rows, (TOKENS, 1), jnp.float32) * math.log(10.0))
    col_scale = jnp.exp(jax.random.uniform(key_cols, (1, D), jnp.float32) * math.log(4.0)) * feature_trend[None, :]
    return (normal_part * row_scale * col_scale).astype(jnp.bfloat16)


def strengthened(result, rng, source, target, blocks, factor):
    owner, partner = [(jnp.arange(result.shape[axis_at]) // (result.shape[axis_at] // blocks)).reshape([-1 if axis == axis_at else 1 for axis in range(result.ndim)]) for axis_at in (source, target)]
    chosen = jax.random.permutation(rng, blocks)[partner]
    strong = (owner == chosen) | (owner == (partner + blocks // 2) % blocks)
    return jnp.where(strong, factor * result, result)


def shard_levels(stream_key, dims, pieces, least, top_value):
    def one(dim, parts):
        steps = jax.random.uniform(jax.random.fold_in(jax.random.fold_in(stream_key, 6), dim), (parts,), jnp.float32, least / len(pieces), top_value / len(pieces))
        return jnp.repeat(jnp.exp(steps), dims[dim] // parts).reshape((-1,) + (1,) * (len(dims) - dim - 1))

    level = one(*pieces[0])
    for cut in pieces[1:]:
        level = level * one(*cut)
    return level


def centred(own_key, shape, scale, reach, shards=(), kind=jnp.bfloat16):
    result = scale * jax.random.normal(own_key, shape, jnp.float32)
    if shards:
        result = result * shard_levels(own_key, shape, shards, -0.22, 0.18)
    return jnp.clip(result, -reach, reach).astype(kind)


def noise_with(rng, dims, deviation, most, cuts, heavy, kind=jnp.bfloat16):
    result = deviation * jax.random.normal(rng, dims, jnp.float32)
    if cuts:
        result = result * shard_levels(rng, dims, cuts, -0.22, 0.18)
    return jnp.clip(strengthened(result, jax.random.fold_in(rng, 3), *heavy), -most, most).astype(kind)


def setup_inputs(seed: int = 0) -> dict:
    keys = jax.random.split(jax.random.key(seed), 7)
    tokens = draw_tokens(jax.random.fold_in(keys[6], 71), 0)
    norm_gain = jnp.clip(1.0 + 0.1 * jax.random.normal(keys[1], (N_REP, D), jnp.float32), 0.5, 1.5).astype(jnp.bfloat16)
    key_weight = noise_with(keys[2], (N_REP, KV_COLS, D), D ** -0.5, 0.3125, ((0, 128), (2, 8)), (0, 1, 128, 5.5))
    key_cotangent = noise_with(keys[3], (TOKENS, KV_COLS), 1.0, 24.0, ((0, 1024),), (0, 1, 1024, 6.0))
    global_fragment = centred(keys[4], (KV_COLS, D), 1.0, 6.0, ((0, 128), (1, 8)), jnp.float32)
    outer_momentum = centred(keys[5], (KV_COLS, D), 0.5, 3.0, ((0, 128), (1, 8)), jnp.float32)
    return {"tokens": tokens, "norm_gain": norm_gain, "key_weight": key_weight, "key_cotangent": key_cotangent, "global_fragment": global_fragment, "outer_momentum": outer_momentum}


rms_eps = 1e-06
inner_rate = 0.3
outer_rate = 0.7
outer_beta = 0.9

def replica_step(running, inputs):
    tok_rows, cot_rows, gain_row, weight_mat = inputs
    tok_float = tok_rows.astype(jnp.float32)
    square_sum = lax.optimization_barrier(jnp.sum(tok_float * tok_float, axis=1, keepdims=True))
    inv_rms = lax.rsqrt(square_sum / D + rms_eps)
    normed = tok_float * inv_rms
    hidden = (normed * gain_row.astype(jnp.float32)).astype(jnp.bfloat16)
    hid_split = hidden.astype(jnp.float32).reshape(TOK_REP, N_FSDP, D // N_FSDP)
    weight_split = weight_mat.astype(jnp.float32).reshape(KV_COLS, N_FSDP, D // N_FSDP)
    partials = jnp.einsum('tgd,kgd->gtk', hid_split, weight_split).astype(jnp.bfloat16)
    partials = lax.optimization_barrier(partials)
    key_out = lax.optimization_barrier(jnp.sum(partials.astype(jnp.float32), axis=0)).astype(jnp.bfloat16)
    hidden_grad = jnp.dot(cot_rows, weight_mat, preferred_element_type=jnp.float32)
    gain_term = lax.optimization_barrier(jnp.sum(hidden_grad * normed, axis=0))
    weight_grad = jnp.dot(cot_rows.T, hidden, preferred_element_type=jnp.float32)
    inner_new = weight_mat.astype(jnp.float32) - inner_rate * weight_grad
    return (running + inner_new, (key_out, gain_term))

def reference(tokens, norm_gain, key_weight, key_cotangent, global_fragment, outer_momentum):
    tok_split = tokens.reshape(N_REP, TOK_REP, D)
    cot_split = key_cotangent.reshape(N_REP, TOK_REP, KV_COLS)
    start_sum = jnp.zeros((KV_COLS, D), jnp.float32)
    summed, (key_out, gain_grad) = lax.scan(replica_step, start_sum, (tok_split, cot_split, norm_gain, key_weight))
    key_out = key_out.reshape(TOKENS, KV_COLS)
    avg_grad = global_fragment - summed / N_REP
    new_momentum = outer_beta * outer_momentum + avg_grad
    new_global = global_fragment - outer_rate * (avg_grad + outer_beta * new_momentum)
    return (key_out, gain_grad, new_global, new_momentum)
```

```python
import jax
import jax.numpy as jnp
from jax import lax
from jax.sharding import Mesh, PartitionSpec as P

D = 4608
N_REP = 128

rms_eps = 1e-06
inner_rate = 0.3
outer_rate = 0.7
outer_beta = 0.9

FSDP = ("x", "yh")
REP = ("yl", "zh", "zl", "core")
SWAP = [(0, 1), (1, 0)]
f32 = jnp.float32
bf16 = jnp.bfloat16


def spread(block):
    return jnp.broadcast_to(block[None], (8,) + block.shape)


def per_device(tokens, norm_gain, key_weight, key_cotangent, global_fragment, outer_momentum):
    tok_float = tokens.astype(f32)
    square_part = jnp.sum(tok_float * tok_float, axis=1).reshape(8, 128)
    square_all = lax.all_to_all(spread(square_part), FSDP, 0, 0)
    cot_all = lax.all_to_all(spread(key_cotangent), FSDP, 0, 0).reshape(1024, 1024)
    square_sum = jnp.sum(square_all, axis=0).reshape(1024)
    inv_rms = lax.rsqrt(square_sum / D + rms_eps)
    normed = tok_float * inv_rms[:, None]
    hidden = (normed * norm_gain[0].astype(f32)).astype(bf16)
    weight = key_weight[0]
    partial_keys = lax.dot_general(
        hidden, weight, (((1,), (1,)), ((), ())), preferred_element_type=f32
    ).astype(bf16)
    key_parts = lax.all_to_all(partial_keys.reshape(8, 128, 1024), FSDP, 0, 0)
    key_out = jnp.sum(key_parts.astype(f32), axis=0).astype(bf16)
    hidden_grad = jnp.dot(cot_all, weight, preferred_element_type=f32)
    gain_grad = jnp.sum(hidden_grad * normed, axis=0)
    weight_grad = lax.dot_general(
        cot_all, hidden, (((0,), (0,)), ((), ())), preferred_element_type=f32
    )
    inner_new = weight.astype(f32) - inner_rate * weight_grad
    core = lax.axis_index("core")
    yl = lax.axis_index("yl")
    total = inner_new.reshape(2, 8, 4, 2, 8, 576)
    mine = lax.dynamic_index_in_dim(total, core, 3, keepdims=False)
    other = lax.dynamic_index_in_dim(total, 1 - core, 3, keepdims=False)
    total = mine + lax.ppermute(other.astype(bf16), "core", SWAP).astype(f32)
    mine = lax.dynamic_index_in_dim(total, yl, 0, keepdims=False)
    other = lax.dynamic_index_in_dim(total, 1 - yl, 0, keepdims=False)
    total = mine + lax.ppermute(other.astype(bf16), "yl", SWAP).astype(f32)
    total = lax.all_to_all(total.astype(bf16).transpose(1, 0, 2, 3), "zl", 0, 0)
    total = jnp.sum(total.astype(f32), axis=0)
    total = lax.all_to_all(total.astype(bf16), "zh", 0, 0)
    summed = jnp.sum(total.astype(f32), axis=0)
    avg_grad = global_fragment - summed / N_REP
    new_momentum = outer_beta * outer_momentum + avg_grad
    new_global = global_fragment - outer_rate * (avg_grad + outer_beta * new_momentum)
    return (key_out, gain_grad[None], new_global, new_momentum)


def solution(mesh):
    fine = Mesh(mesh.devices.reshape(2, 8, 4, 2, 4, 2), REP + FSDP)
    return jax.shard_map(
        per_device,
        mesh=fine,
        in_specs=(
            P(REP, FSDP),
            P(REP, FSDP),
            P(REP, None, FSDP),
            P(REP + FSDP, None),
            P(REP, FSDP),
            P(REP, FSDP),
        ),
        out_specs=(P(REP + FSDP, None), P(REP, FSDP), P(REP, FSDP), P(REP, FSDP)),
        check_vma=False,
    )
```

```python
import functools

import jax
import jax.numpy as jnp
from jax import lax
from jax.experimental import pallas as pl
from jax.experimental.pallas import tpu as pltpu
from jax.sharding import Mesh, PartitionSpec as P

D = 4608
N_REP = 128
FEAT = 576

rms_eps = 1e-06
inner_rate = 0.3
outer_rate = 0.7
outer_beta = 0.9

FSDP = ("x", "yh")
REP = ("yl", "zh", "zl", "core")
ZC = ("zh", "zl", "core")
SWAP = [(0, 1), (1, 0)]
f32 = jnp.float32
bf16 = jnp.bfloat16
S = jax.ShapeDtypeStruct
PARAMS = pltpu.CompilerParams(vmem_limit_bytes=40 * 2**20)


def z_shift(delta):
    pairs = []
    for z in range(32):
        for core, sign in ((0, 1), (1, -1)):
            pairs.append((z * 2 + core, (z + sign * delta) % 32 * 2 + core))
    return pairs


def pack_kernel(cot_ref, tok_ref, first_ref, second_ref, turned):
    yl = lax.axis_index("yl")
    turned[...] = cot_ref[...].astype(f32).T.reshape(2, 32, 2, 8, 128)
    rows = []
    for j in range(8):
        tok = tok_ref[:, j * 128 : (j + 1) * 128].astype(f32)
        rows.append(jnp.sum(tok * tok, axis=0, keepdims=True))
    square = jnp.concatenate(rows, axis=0)
    high = square.astype(bf16).astype(f32)
    middle = (square - high).astype(bf16).astype(f32)
    low = square - high - middle
    tail = jnp.concatenate([high, middle, low, jnp.zeros_like(low)], axis=0).astype(bf16)
    other, mine = turned[1 - yl], turned[yl]
    for core in range(2):
        to_other = other[:, core].reshape(256, 128).astype(bf16)
        to_mine = mine[:, core].reshape(256, 128).astype(bf16)
        for peer in range(8):
            first_ref[core * 8 + peer, 0:256] = to_other
            first_ref[core * 8 + peer, 256:288] = tail
            second_ref[core * 8 + peer] = to_mine


def product(got_ref, core, hidden):
    cot = jnp.concatenate([got_ref[core * 8 + g, 0:256] for g in range(8)], axis=1)
    return lax.dot_general(cot, hidden, (((1,), (1,)), ((), ())), preferred_element_type=f32)


def first_kernel(
    got_ref, tok_ref, tok_sib_ref, gain_ref, gain_sib_ref, w_ref, w_sib_ref,
    send_ref, hid_ref, hid_sib_ref, part_ref, part_sib_ref,
):
    core = lax.axis_index("core")
    yl = lax.axis_index("yl")
    new = jnp.zeros((256, FEAT), f32)
    for which, tok, gain, weight, hid_out, part in (
        (core, tok_ref, gain_ref, w_ref, hid_ref, part_ref),
        (1 - core, tok_sib_ref, gain_sib_ref, w_sib_ref, hid_sib_ref, part_sib_ref),
    ):
        square = jnp.zeros((8, 128), f32)
        for g in range(8):
            tail = got_ref[which * 8 + g, 256:288].astype(f32)
            square += tail[0:8] + (tail[8:16] + tail[16:24])
        inv_rms = lax.rsqrt(square / D + rms_eps)
        for j in range(8):
            normed = tok[:, j * 128 : (j + 1) * 128].astype(f32) * inv_rms[j : j + 1]
            hid_out[:, j * 128 : (j + 1) * 128] = (normed * gain[...]).astype(bf16)
        grad = product(got_ref, which, hid_out[...])
        w = weight[1 - yl].astype(f32)
        part[...] = jnp.sum(w * grad, axis=0, keepdims=True)
        new += w - inner_rate * grad
    send_ref[...] = new.astype(bf16)


def second_kernel(
    got_ref, hid_ref, hid_sib_ref, w_ref, w_sib_ref, arrived_ref, part_ref, part_sib_ref,
    keep_ref, plus_ref, minus_ref, gain_ref, gain_sib_ref, total,
):
    core = lax.axis_index("core")
    yl = lax.axis_index("yl")
    z = lax.axis_index("zh") * 4 + lax.axis_index("zl")
    sign = 1 - 2 * core
    new = arrived_ref[...].astype(f32)
    for which, hid, weight, part, out in (
        (core, hid_ref, w_ref, part_ref, gain_ref),
        (1 - core, hid_sib_ref, w_sib_ref, part_sib_ref, gain_sib_ref),
    ):
        grad = product(got_ref, which, hid[...])
        w = weight[yl].astype(f32)
        out[...] = part[...] + jnp.sum(w * grad, axis=0, keepdims=True)
        new += w - inner_rate * grad
    total[...] = new.reshape(32, 8, FEAT)

    def block(offset):
        return total[(z + sign * offset + 64) % 32]

    for i in range(11):
        at = 3 * i - 12
        keep_ref[i] = block(at)
        minus_ref[i] = block(at - 1).astype(bf16)
        if i < 10:
            plus_ref[i] = block(at + 1).astype(bf16)


def third_kernel(keep_ref, plus_ref, minus_ref, keep_out, plus_out, minus_out):
    total = []
    for i in range(11):
        value = keep_ref[i] + minus_ref[i].astype(f32)
        if i < 10:
            value += plus_ref[i].astype(f32)
        total.append(value)
    for c in range(4):
        keep_out[c] = total[3 * c + 1]
        minus_out[c] = total[3 * c].astype(bf16)
        if c < 3:
            plus_out[c] = total[3 * c + 2].astype(bf16)


def fourth_kernel(keep_ref, plus_ref, minus_ref, keep_out, back_out, on_out, far_out):
    total = []
    for c in range(4):
        value = keep_ref[c] + minus_ref[c].astype(f32)
        if c < 3:
            value += plus_ref[c].astype(f32)
        total.append(value)
    back_out[0] = total[0].astype(bf16)
    keep_out[...] = total[1]
    on_out[0] = total[2].astype(bf16)
    far_out[0] = total[3].astype(bf16)


def per_device(tokens, norm_gain, key_weight, key_cotangent, global_fragment, outer_momentum):
    core = lax.axis_index("core")
    tok = tokens.T
    first, second = pl.pallas_call(
        pack_kernel,
        out_shape=(S((16, 288, 128), bf16), S((16, 256, 128), bf16)),
        scratch_shapes=[pltpu.VMEM((2, 32, 2, 8, 128), f32)],
        compiler_params=PARAMS,
        name="pack",
    )(key_cotangent, tok)
    got_first = lax.all_to_all(first, ("core",) + FSDP, 0, 0)

    weight_t = key_weight[0].T
    blocks = key_weight.reshape(2, 32, 2, 8, FEAT)
    w_mine = lax.dynamic_index_in_dim(blocks, core, 2, keepdims=False).reshape(2, 256, FEAT)
    w_other = lax.dynamic_index_in_dim(blocks, 1 - core, 2, keepdims=False).reshape(2, 256, FEAT)
    gain = norm_gain.astype(f32).reshape(FEAT, 1)
    tok_sib = lax.ppermute(tok, "core", SWAP)
    gain_sib = lax.ppermute(gain, "core", SWAP)
    w_sib = lax.ppermute(w_other, "core", SWAP)

    send, hid, hid_sib, part, part_sib = pl.pallas_call(
        first_kernel,
        out_shape=(
            S((256, FEAT), bf16), S((FEAT, 1024), bf16), S((FEAT, 1024), bf16),
            S((1, FEAT), f32), S((1, FEAT), f32),
        ),
        compiler_params=PARAMS,
        name="first",
    )(got_first, tok, tok_sib, gain, gain_sib, w_mine, w_sib)
    arrived = lax.ppermute(send, "yl", SWAP)
    second, _ = lax.optimization_barrier((second, got_first))
    got_second = lax.all_to_all(second, ("core",) + FSDP, 0, 0)

    partial_keys = lax.dot_general(
        hid, weight_t, (((0,), (0,)), ((), ())), preferred_element_type=f32
    ).astype(bf16)

    keep, plus, minus, part, part_sib = pl.pallas_call(
        second_kernel,
        out_shape=(
            S((11, 8, FEAT), f32), S((10, 8, FEAT), bf16), S((11, 8, FEAT), bf16),
            S((1, FEAT), f32), S((1, FEAT), f32),
        ),
        scratch_shapes=[pltpu.VMEM((32, 8, FEAT), f32)],
        compiler_params=PARAMS,
        name="second",
    )(got_second, hid, hid_sib, w_mine, w_sib, arrived, part, part_sib)

    partial_keys, _ = lax.optimization_barrier((partial_keys, got_second))
    key_parts = lax.all_to_all(partial_keys.reshape(8, 128, 1024), FSDP, 0, 0)
    key_out = jnp.sum(key_parts.astype(f32), axis=0).astype(bf16)

    plus = lax.ppermute(plus, ZC, z_shift(1))
    minus = lax.ppermute(minus, ZC, z_shift(-1))
    keep, plus, minus = pl.pallas_call(
        third_kernel,
        out_shape=(S((4, 8, FEAT), f32), S((3, 8, FEAT), bf16), S((4, 8, FEAT), bf16)),
        compiler_params=PARAMS,
        name="third",
    )(keep, plus, minus)
    plus = lax.ppermute(plus, ZC, z_shift(3))
    minus = lax.ppermute(minus, ZC, z_shift(-3))
    one = S((1, 8, FEAT), bf16)
    keep, back, on, far = pl.pallas_call(
        fourth_kernel,
        out_shape=(S((8, FEAT), f32), one, one, one),
        compiler_params=PARAMS,
        name="fourth",
    )(keep, plus, minus)
    far = lax.ppermute(far, ZC, z_shift(18))
    on = lax.ppermute(on, ZC, z_shift(9))
    back = lax.ppermute(back, ZC, z_shift(-9))
    gain_grad = part + lax.ppermute(part_sib, "core", SWAP)
    gain_grad = gain_grad / norm_gain.astype(f32)
    summed = keep + far[0].astype(f32) + on[0].astype(f32) + back[0].astype(f32)
    avg_grad = global_fragment - summed / N_REP
    new_momentum = outer_beta * outer_momentum + avg_grad
    new_global = global_fragment - outer_rate * (avg_grad + outer_beta * new_momentum)
    return (key_out, gain_grad, new_global, new_momentum)


def solution(mesh):
    fine = Mesh(mesh.devices.reshape(2, 8, 4, 2, 4, 2), REP + FSDP)
    return jax.shard_map(
        per_device,
        mesh=fine,
        in_specs=(
            P(REP, FSDP),
            P(REP, FSDP),
            P(REP, None, FSDP),
            P(REP + FSDP, None),
            P(REP, FSDP),
            P(REP, FSDP),
        ),
        out_specs=(P(REP + FSDP, None), P(REP, FSDP), P(REP, FSDP), P(REP, FSDP)),
        check_vma=False,
    )
```

```python
import jax
import jax.numpy as jnp
from jax import lax
from jax.experimental import pallas as pl
from jax.experimental.pallas import tpu as pltpu
from jax.sharding import Mesh, PartitionSpec as P

D = 4608
N_REP = 128
FEAT = 576

rms_eps = 1e-06
inner_rate = 0.3
outer_rate = 0.7
outer_beta = 0.9

FSDP = ("x", "yh")
REP = ("yl", "zh", "zl", "core")
SWAP = [(0, 1), (1, 0)]
f32 = jnp.float32
bf16 = jnp.bfloat16
S = jax.ShapeDtypeStruct
PARAMS = pltpu.CompilerParams(vmem_limit_bytes=24 * 2**20)


HBM = pl.BlockSpec(memory_space=pltpu.HBM)
CHEAP = pl.CostEstimate(flops=1000, bytes_accessed=1000, transcendentals=0)
ANY = pl.BlockSpec(memory_space=pl.ANY)
VMEM = pl.BlockSpec(memory_space=pltpu.VMEM)


def far(array):
    return pltpu.with_memory_space_constraint(array, pltpu.HBM)


def partner(bits):
    return [(i, i ^ bits) for i in range(8)]


def turned_columns(cot, turned):
    turned[...] = cot[...].astype(f32).T.reshape(2, 32, 2, 8, 128)


def send_out(buffer, out_ref, sems):
    copies = []
    for core in range(2):
        for peer in range(8):
            at = core * 8 + peer
            copies.append(pltpu.make_async_copy(buffer.at[core], out_ref.at[at], sems.at[at]))
            copies[-1].start()
    for copy in copies:
        copy.wait()


def pack_first_kernel(cot_hbm, tok_hbm, out_ref, cot, tok, turned, buffer, sems, in_sems):
    yl = lax.axis_index("yl")
    cot_copy = pltpu.make_async_copy(cot_hbm, cot, in_sems.at[0])
    tok_copy = pltpu.make_async_copy(tok_hbm, tok, in_sems.at[1])
    cot_copy.start()
    tok_copy.start()
    cot_copy.wait()
    turned_columns(cot, turned)
    block = turned[1 - yl]
    for core in range(2):
        buffer[core, 0:256] = block[:, core].reshape(256, 128).astype(bf16)
    tok_copy.wait()
    rows = []
    for j in range(8):
        part = tok[:, j * 128 : (j + 1) * 128].astype(f32)
        rows.append(jnp.sum(part * part, axis=0, keepdims=True))
    square = jnp.concatenate(rows, axis=0)
    high = square.astype(bf16).astype(f32)
    middle = (square - high).astype(bf16).astype(f32)
    low = square - high - middle
    tail = jnp.concatenate([high, middle, low, jnp.zeros_like(low)], axis=0).astype(bf16)
    for core in range(2):
        buffer[core, 256:288] = tail
    send_out(buffer, out_ref, sems)


def pack_second_kernel(cot, w_sib, out_ref, turned, buffer, sems):
    turned_columns(cot, turned)
    block = turned[lax.axis_index("yl")]
    for core in range(2):
        buffer[core] = block[:, core].reshape(256, 128).astype(bf16)
    send_out(buffer, out_ref, sems)


def weight_kernel(wt_ref, gain_ref, mine_ref, other_ref, turned):
    core = lax.axis_index("core")
    turned[...] = wt_ref[...].astype(f32).T.reshape(64, 2, 8, FEAT)
    gain = jnp.broadcast_to(gain_ref[...].astype(f32), (16, FEAT)).astype(bf16)
    for which, out in ((core, mine_ref), (1 - core, other_ref)):
        out[0:512] = turned[:, which].reshape(512, FEAT).astype(bf16)
        out[512:528] = gain


def product(got, hidden):
    cot = jnp.concatenate([got[g, 0:256] for g in range(8)], axis=1)
    return lax.dot_general(cot, hidden, (((1,), (1,)), ((), ())), preferred_element_type=f32)


def half_rows(which):
    return pl.ds(pl.multiple_of(which * 256, 256), 256)


def eight(which):
    return pl.ds(which * 8, 8)


def start_all(pairs, sems):
    copies = [pltpu.make_async_copy(src, dst, sems.at[i]) for i, (src, dst) in enumerate(pairs)]
    for copy in copies:
        copy.start()
    return copies


def first_kernel(
    got_hbm, tok_hbm, tok_sib_hbm, w_hbm, w_sib_hbm,
    send_ref, hid_hbm, hid_sib_hbm, part_ref, part_sib_ref,
    got, tok, weight, gains, hid, sems,
):
    core = lax.axis_index("core")
    yl = lax.axis_index("yl")
    copies = start_all(
        [
            (got_hbm.at[eight(core)], got.at[0]),
            (tok_hbm, tok.at[0]),
            (w_hbm.at[pl.ds(512, 16)], gains.at[0]),
            (w_hbm.at[half_rows(1 - yl)], weight.at[0]),
            (got_hbm.at[eight(1 - core)], got.at[1]),
            (tok_sib_hbm, tok.at[1]),
            (w_sib_hbm.at[pl.ds(512, 16)], gains.at[1]),
            (w_sib_hbm.at[half_rows(1 - yl)], weight.at[1]),
        ],
        sems,
    )
    new = jnp.zeros((256, FEAT), f32)
    out_copies = []
    for slot, (hid_out, part) in enumerate(((hid_hbm, part_ref), (hid_sib_hbm, part_sib_ref))):
        copies[slot * 4].wait()
        square = jnp.zeros((8, 128), f32)
        for g in range(8):
            tail = got[slot, g, 256:288].astype(f32)
            square += tail[0:8] + (tail[8:16] + tail[16:24])
        inv_rms = lax.rsqrt(square / D + rms_eps)
        copies[slot * 4 + 2].wait()
        gain = gains[slot].astype(f32)[0:8].T[:, 0:1]
        copies[slot * 4 + 1].wait()
        for j in range(8):
            at = slice(j * 128, (j + 1) * 128)
            normed = tok[slot, :, at].astype(f32) * inv_rms[j : j + 1]
            hid[slot, :, at] = (normed * gain).astype(bf16)
        out_copies.append(pltpu.make_async_copy(hid.at[slot], hid_out, sems.at[8 + slot]))
        out_copies[-1].start()
        grad = product(got.at[slot], hid[slot])
        copies[slot * 4 + 3].wait()
        w = weight[slot].astype(f32)
        part[...] = jnp.sum(w * grad, axis=0, keepdims=True)
        new += w - inner_rate * grad
    send_ref[...] = new.astype(bf16)
    for copy in out_copies:
        copy.wait()


def second_kernel(
    got_hbm, hid_hbm, hid_sib_hbm, w_hbm, w_sib_hbm, arrived_hbm, part_ref, part_sib_ref,
    out_ref, gain_ref, gain_sib_ref,
    got, hid, weight, arrived, sems,
):
    core = lax.axis_index("core")
    yl = lax.axis_index("yl")
    copies = start_all(
        [
            (hid_hbm, hid.at[0]),
            (got_hbm.at[eight(core)], got.at[0]),
            (w_hbm.at[half_rows(yl)], weight.at[0]),
            (hid_sib_hbm, hid.at[1]),
            (got_hbm.at[eight(1 - core)], got.at[1]),
            (w_sib_hbm.at[half_rows(yl)], weight.at[1]),
            (arrived_hbm, arrived),
        ],
        sems,
    )
    new = jnp.zeros((256, FEAT), f32)
    for slot, (part, out) in enumerate(((part_ref, gain_ref), (part_sib_ref, gain_sib_ref))):
        copies[slot * 3].wait()
        copies[slot * 3 + 1].wait()
        grad = product(got.at[slot], hid[slot])
        copies[slot * 3 + 2].wait()
        w = weight[slot].astype(f32)
        out[...] = part[...] + jnp.sum(w * grad, axis=0, keepdims=True)
        new += w - inner_rate * grad
    copies[6].wait()
    total = (new + arrived[...].astype(f32)).reshape(8, 4, 8, FEAT)
    for zl in range(4):
        out_ref[zl] = total[:, zl].reshape(64, FEAT).astype(bf16)


def keys_kernel(hid_ref, wt_ref, after_ref, *outs):
    me = lax.axis_index("x") * 2 + lax.axis_index("yh")
    for bit, out in enumerate(outs):
        group = me ^ bit
        hid = hid_ref[:, pl.ds(pl.multiple_of(group * 128, 128), 128)]
        out[...] = lax.dot_general(
            hid, wt_ref[...], (((0,), (0,)), ((), ())), preferred_element_type=f32
        ).astype(bf16)


def per_device(tokens, norm_gain, key_weight, key_cotangent, global_fragment, outer_momentum):
    tok = tokens.T
    weight_t = key_weight[0].T
    first = pl.pallas_call(
        pack_first_kernel,
        out_shape=pltpu.HBM((16, 288, 128), bf16),
        in_specs=[HBM, HBM],
        out_specs=HBM,
        scratch_shapes=[
            pltpu.VMEM((128, 1024), bf16),
            pltpu.VMEM((FEAT, 1024), bf16),
            pltpu.VMEM((2, 32, 2, 8, 128), f32),
            pltpu.VMEM((2, 288, 128), bf16),
            pltpu.SemaphoreType.DMA((16,)),
            pltpu.SemaphoreType.DMA((2,)),
        ],
        compiler_params=PARAMS,
        name="pack_first",
    )(far(key_cotangent), far(tok))
    got_first = lax.all_to_all(first, ("core",) + FSDP, 0, 0)

    tok_sib = lax.ppermute(tok, "core", SWAP)
    w_mine, w_other = pl.pallas_call(
        weight_kernel,
        out_shape=(S((528, FEAT), bf16), S((528, FEAT), bf16)),
        scratch_shapes=[pltpu.VMEM((64, 2, 8, FEAT), f32)],
        compiler_params=PARAMS,
        cost_estimate=CHEAP,
        name="weights",
    )(weight_t, norm_gain)
    w_sib = lax.ppermute(w_other, "core", SWAP)
    second = pl.pallas_call(
        pack_second_kernel,
        out_shape=pltpu.HBM((16, 256, 128), bf16),
        in_specs=[VMEM, ANY],
        out_specs=HBM,
        scratch_shapes=[
            pltpu.VMEM((2, 32, 2, 8, 128), f32),
            pltpu.VMEM((2, 256, 128), bf16),
            pltpu.SemaphoreType.DMA((16,)),
        ],
        compiler_params=PARAMS,
        cost_estimate=CHEAP,
        name="pack_second",
    )(key_cotangent, w_sib)

    send, hid, hid_sib, part, part_sib = pl.pallas_call(
        first_kernel,
        out_shape=(
            S((256, FEAT), bf16), pltpu.HBM((FEAT, 1024), bf16), pltpu.HBM((FEAT, 1024), bf16),
            S((1, FEAT), f32), S((1, FEAT), f32),
        ),
        in_specs=[HBM] * 5,
        out_specs=(VMEM, HBM, HBM, VMEM, VMEM),
        scratch_shapes=[
            pltpu.VMEM((2, 8, 288, 128), bf16),
            pltpu.VMEM((2, FEAT, 1024), bf16),
            pltpu.VMEM((2, 256, FEAT), bf16),
            pltpu.VMEM((2, 16, FEAT), bf16),
            pltpu.VMEM((2, FEAT, 1024), bf16),
            pltpu.SemaphoreType.DMA((10,)),
        ],
        compiler_params=PARAMS,
        name="first",
    )(far(got_first), far(tok), far(tok_sib), far(w_mine), far(w_sib))
    arrived = lax.ppermute(send, "yl", SWAP)
    got_second = lax.all_to_all(second, ("core",) + FSDP, 0, 0)

    payload, part, part_sib = pl.pallas_call(
        second_kernel,
        out_shape=(S((4, 64, FEAT), bf16), S((1, FEAT), f32), S((1, FEAT), f32)),
        in_specs=[HBM] * 6 + [VMEM] * 2,
        scratch_shapes=[
            pltpu.VMEM((2, 8, 256, 128), bf16),
            pltpu.VMEM((2, FEAT, 1024), bf16),
            pltpu.VMEM((2, 256, FEAT), bf16),
            pltpu.VMEM((256, FEAT), bf16),
            pltpu.SemaphoreType.DMA((7,)),
        ],
        compiler_params=PARAMS,
        name="second",
    )(
        far(got_second), far(hid), far(hid_sib), far(w_mine), far(w_sib), far(arrived), part, part_sib
    )

    keys = pl.pallas_call(
        keys_kernel,
        out_shape=tuple(S((128, 1024), bf16) for _ in range(8)),
        in_specs=[VMEM, VMEM, ANY],
        compiler_params=PARAMS,
        name="keys",
    )(hid, weight_t, payload)
    pieces = [lax.ppermute(keys[bit], FSDP, partner(bit)) for bit in range(1, 8)]
    z_parts = lax.all_to_all(payload, "zl", 0, 0)
    z_sum = jnp.sum(z_parts.astype(f32), axis=0).astype(bf16).reshape(8, 8, FEAT)
    z_parts = lax.all_to_all(z_sum, "zh", 0, 0)
    summed = jnp.sum(z_parts.astype(f32), axis=0)

    gain_grad = part + lax.ppermute(part_sib, "core", SWAP)
    gain_grad = gain_grad / norm_gain.astype(f32)
    avg_grad = global_fragment - summed / N_REP
    new_momentum = outer_beta * outer_momentum + avg_grad
    new_global = global_fragment - outer_rate * (avg_grad + outer_beta * new_momentum)
    key_out = keys[0].astype(f32)
    for piece in pieces:
        key_out += piece.astype(f32)
    return (key_out.astype(bf16), gain_grad, new_global, new_momentum)


def solution(mesh):
    fine = Mesh(mesh.devices.reshape(2, 8, 4, 2, 4, 2), REP + FSDP)
    return jax.shard_map(
        per_device,
        mesh=fine,
        in_specs=(
            P(REP, FSDP),
            P(REP, FSDP),
            P(REP, None, FSDP),
            P(REP + FSDP, None),
            P(REP, FSDP),
            P(REP, FSDP),
        ),
        out_specs=(P(REP + FSDP, None), P(REP, FSDP), P(REP, FSDP), P(REP, FSDP)),
        check_vma=False,
    )
```

```python
import jax
import jax.numpy as jnp
from jax import lax
from jax.experimental import pallas as pl
from jax.experimental.pallas import tpu as pltpu
from jax.sharding import Mesh, PartitionSpec as P

D = 4608
N_REP = 128
FEAT = 576

rms_eps = 1e-06
inner_rate = 0.3
outer_rate = 0.7
outer_beta = 0.9

FSDP = ("x", "yh")
REP = ("yl", "zh", "zl", "core")
ZC = ("zh", "zl", "core")
SWAP = [(0, 1), (1, 0)]
f32 = jnp.float32
bf16 = jnp.bfloat16
S = jax.ShapeDtypeStruct
PARAMS = pltpu.CompilerParams(vmem_limit_bytes=24 * 2**20)


HBM = pl.BlockSpec(memory_space=pltpu.HBM)
CHEAP = pl.CostEstimate(flops=1000, bytes_accessed=1000, transcendentals=0)
ANY = pl.BlockSpec(memory_space=pl.ANY)
VMEM = pl.BlockSpec(memory_space=pltpu.VMEM)


def far(array):
    return pltpu.with_memory_space_constraint(array, pltpu.HBM)


def z_shift(delta):
    pairs = []
    for z in range(32):
        for core, sign in ((0, 1), (1, -1)):
            pairs.append((z * 2 + core, (z + sign * delta) % 32 * 2 + core))
    return pairs


def send_out(buffer, out_ref, sems):
    copies = []
    for core in range(2):
        for peer in range(8):
            at = core * 8 + peer
            copies.append(pltpu.make_async_copy(buffer.at[core], out_ref.at[at], sems.at[at]))
            copies[-1].start()
    for copy in copies:
        copy.wait()


def pack_kernel(cot_hbm, tok_hbm, out_ref, cot, tok, buffer, sems, in_sems):
    cot_copy = pltpu.make_async_copy(cot_hbm, cot, in_sems.at[0])
    tok_copy = pltpu.make_async_copy(tok_hbm, tok, in_sems.at[1])
    cot_copy.start()
    tok_copy.start()
    cot_copy.wait()
    turned = cot[...].astype(f32).T.reshape(64, 2, 8, 128)
    for core in range(2):
        buffer[core, 0:512] = turned[:, core].reshape(512, 128).astype(bf16)
    tok_copy.wait()
    rows = []
    for j in range(8):
        part = tok[:, j * 128 : (j + 1) * 128].astype(f32)
        rows.append(jnp.sum(part * part, axis=0, keepdims=True))
    square = jnp.concatenate(rows, axis=0)
    high = square.astype(bf16).astype(f32)
    middle = (square - high).astype(bf16).astype(f32)
    low = square - high - middle
    tail = jnp.concatenate([high, middle, low, jnp.zeros_like(low)], axis=0).astype(bf16)
    for core in range(2):
        buffer[core, 512:544] = tail
    send_out(buffer, out_ref, sems)


def weight_kernel(wt_ref, gain_ref, mine_ref, other_ref, turned):
    core = lax.axis_index("core")
    turned[...] = wt_ref[...].astype(f32).T.reshape(64, 2, 8, FEAT)
    gain = jnp.broadcast_to(gain_ref[...].astype(f32), (16, FEAT)).astype(bf16)
    for which, out in ((core, mine_ref), (1 - core, other_ref)):
        out[0:512] = turned[:, which].reshape(512, FEAT).astype(bf16)
        out[512:528] = gain


def product(got, hidden):
    cot = jnp.concatenate([got[g, 0:512] for g in range(8)], axis=1)
    return lax.dot_general(cot, hidden, (((1,), (1,)), ((), ())), preferred_element_type=f32)


def eight(which):
    return pl.ds(which * 8, 8)


def start_all(pairs, sems):
    copies = [pltpu.make_async_copy(src, dst, sems.at[i]) for i, (src, dst) in enumerate(pairs)]
    for copy in copies:
        copy.start()
    return copies


def grad_kernel(
    got_hbm, tok_hbm, tok_sib_hbm, w_hbm, w_sib_hbm,
    send_ref, keep_ref, hid_hbm, part_ref, part_sib_ref,
    got, tok, weight, hid, sems,
):
    core = lax.axis_index("core")
    yl = lax.axis_index("yl")
    copies = start_all(
        [
            (got_hbm.at[eight(core)], got.at[0]),
            (tok_hbm, tok.at[0]),
            (w_hbm, weight.at[0]),
            (got_hbm.at[eight(1 - core)], got.at[1]),
            (tok_sib_hbm, tok.at[1]),
            (w_sib_hbm, weight.at[1]),
        ],
        sems,
    )
    new = jnp.zeros((512, FEAT), f32)
    hid_copy = pltpu.make_async_copy(hid.at[0], hid_hbm, sems.at[6])
    for slot, part in enumerate((part_ref, part_sib_ref)):
        copies[slot * 3].wait()
        square = jnp.zeros((8, 128), f32)
        for g in range(8):
            tail = got[slot, g, 512:544].astype(f32)
            square += tail[0:8] + (tail[8:16] + tail[16:24])
        inv_rms = lax.rsqrt(square / D + rms_eps)
        copies[slot * 3 + 1].wait()
        copies[slot * 3 + 2].wait()
        gain = weight[slot, 512:528].astype(f32)[0:8].T[:, 0:1]
        for j in range(8):
            at = slice(j * 128, (j + 1) * 128)
            normed = tok[slot, :, at].astype(f32) * inv_rms[j : j + 1]
            hid[slot, :, at] = (normed * gain).astype(bf16)
        if slot == 0:
            hid_copy.start()
        grad = product(got.at[slot], hid[slot])
        w = weight[slot, 0:512].astype(f32)
        part[...] = jnp.sum(w * grad, axis=0, keepdims=True)
        new += w - inner_rate * grad

    @pl.when(yl == 0)
    def _():
        keep_ref[...] = new[0:256]
        send_ref[...] = new[256:512].astype(bf16)

    @pl.when(yl == 1)
    def _():
        keep_ref[...] = new[256:512]
        send_ref[...] = new[0:256].astype(bf16)

    hid_copy.wait()


def split_kernel(keep_in, arrived, keep, plus, minus, twice, total):
    core = lax.axis_index("core")
    z = lax.axis_index("zh") * 4 + lax.axis_index("zl")
    sign = 1 - 2 * core
    total[...] = (keep_in[...] + arrived[...].astype(f32)).reshape(32, 8, FEAT)

    def block(offset):
        return total[(z + sign * offset + 64) % 32]

    for i in range(8):
        keep[i] = block(4 * (i - 3))
        minus[i] = block(4 * (i - 3) - 1).astype(bf16)
        plus[i] = block(4 * (i - 4) + 1).astype(bf16)
        twice[i] = block(4 * (i - 4) + 2).astype(bf16)


def middle_kernel(keep, plus, minus, twice, keep_out, plus_out, minus_out):
    total = []
    for i in range(9):
        value = jnp.zeros((8, FEAT), f32)
        if i > 0:
            value += keep[i - 1] + minus[i - 1].astype(f32)
        if i < 8:
            value += plus[i].astype(f32) + twice[i].astype(f32)
        total.append(value)
    for c in range(3):
        minus_out[c] = total[3 * c].astype(bf16)
        keep_out[c] = total[3 * c + 1]
        plus_out[c] = total[3 * c + 2].astype(bf16)


def last_kernel(keep, plus, minus, keep_out, back_out, on_out):
    total = [keep[c] + plus[c].astype(f32) + minus[c].astype(f32) for c in range(3)]
    back_out[0] = total[0].astype(bf16)
    keep_out[...] = total[1]
    on_out[0] = total[2].astype(bf16)


def keys_kernel(hid_ref, wt_ref, out_ref):
    for group in range(8):
        hid = hid_ref[:, group * 128 : (group + 1) * 128]
        out_ref[group] = lax.dot_general(
            hid, wt_ref[...], (((0,), (0,)), ((), ())), preferred_element_type=f32
        ).astype(bf16)


def pass_kernel(array, after, also, out):
    pass


def per_device(tokens, norm_gain, key_weight, key_cotangent, global_fragment, outer_momentum):
    tok = tokens.T
    weight_t = key_weight[0].T
    packed = pl.pallas_call(
        pack_kernel,
        out_shape=pltpu.HBM((16, 544, 128), bf16),
        in_specs=[HBM, HBM],
        out_specs=HBM,
        scratch_shapes=[
            pltpu.VMEM((128, 1024), bf16),
            pltpu.VMEM((FEAT, 1024), bf16),
            pltpu.VMEM((2, 544, 128), bf16),
            pltpu.SemaphoreType.DMA((16,)),
            pltpu.SemaphoreType.DMA((2,)),
        ],
        compiler_params=PARAMS,
        name="pack",
    )(far(key_cotangent), far(tok))
    got = lax.all_to_all(packed, ("core",) + FSDP, 0, 0)

    tok_sib = lax.ppermute(tok, "core", SWAP)
    w_mine, w_other = pl.pallas_call(
        weight_kernel,
        out_shape=(S((528, FEAT), bf16), S((528, FEAT), bf16)),
        scratch_shapes=[pltpu.VMEM((64, 2, 8, FEAT), f32)],
        compiler_params=PARAMS,
        cost_estimate=CHEAP,
        name="weights",
    )(weight_t, norm_gain)
    w_sib = lax.ppermute(w_other, "core", SWAP)

    send, keep, hid, part, part_sib = pl.pallas_call(
        grad_kernel,
        out_shape=(
            S((256, FEAT), bf16), S((256, FEAT), f32), pltpu.HBM((FEAT, 1024), bf16),
            S((1, FEAT), f32), S((1, FEAT), f32),
        ),
        in_specs=[ANY] + [HBM] * 4,
        out_specs=(VMEM, VMEM, HBM, VMEM, VMEM),
        scratch_shapes=[
            pltpu.VMEM((2, 8, 544, 128), bf16),
            pltpu.VMEM((2, FEAT, 1024), bf16),
            pltpu.VMEM((2, 528, FEAT), bf16),
            pltpu.VMEM((2, FEAT, 1024), bf16),
            pltpu.SemaphoreType.DMA((7,)),
        ],
        compiler_params=PARAMS,
        name="grad",
    )(got, far(tok), far(tok_sib), far(w_mine), far(w_sib))
    arrived = lax.ppermute(send, "yl", SWAP)
    part_sib = lax.ppermute(part_sib, "core", SWAP)

    keys = pl.pallas_call(
        keys_kernel,
        out_shape=pltpu.HBM((8, 128, 1024), bf16),
        out_specs=VMEM,
        compiler_params=PARAMS,
        name="keys",
    )(hid, weight_t)

    eight_blocks = S((8, 8, FEAT), bf16)
    three = S((3, 8, FEAT), bf16)
    one = S((1, 8, FEAT), bf16)
    keep, plus, minus, twice = pl.pallas_call(
        split_kernel,
        out_shape=(S((8, 8, FEAT), f32), eight_blocks, eight_blocks, eight_blocks),
        scratch_shapes=[pltpu.VMEM((32, 8, FEAT), f32)],
        compiler_params=PARAMS,
        name="split",
    )(keep, arrived)
    keys = pl.pallas_call(
        pass_kernel,
        out_shape=pltpu.HBM((8, 128, 1024), bf16),
        in_specs=[HBM, ANY, ANY],
        out_specs=HBM,
        input_output_aliases={0: 0},
        compiler_params=PARAMS,
        name="pass_on",
    )(keys, plus, part_sib)
    key_parts = lax.all_to_all(keys, FSDP, 0, 0)

    plus = lax.ppermute(plus, ZC, z_shift(1))
    minus = lax.ppermute(minus, ZC, z_shift(-1))
    twice = lax.ppermute(twice, ZC, z_shift(2))
    keep, plus, minus = pl.pallas_call(
        middle_kernel,
        out_shape=(S((3, 8, FEAT), f32), three, three),
        compiler_params=PARAMS,
        name="middle",
    )(keep, plus, minus, twice)
    plus = lax.ppermute(plus, ZC, z_shift(4))
    minus = lax.ppermute(minus, ZC, z_shift(-4))
    keep, back, on = pl.pallas_call(
        last_kernel,
        out_shape=(S((8, FEAT), f32), one, one),
        compiler_params=PARAMS,
        name="last",
    )(keep, plus, minus)
    on = lax.ppermute(on, ZC, z_shift(12))
    back = lax.ppermute(back, ZC, z_shift(-12))
    summed = keep + on[0].astype(f32) + back[0].astype(f32)

    gain_grad = (part + part_sib) / norm_gain.astype(f32)
    avg_grad = global_fragment - summed / N_REP
    new_momentum = outer_beta * outer_momentum + avg_grad
    new_global = global_fragment - outer_rate * (avg_grad + outer_beta * new_momentum)
    key_out = jnp.sum(key_parts.astype(f32), axis=0).astype(bf16)
    return (key_out, gain_grad, new_global, new_momentum)


def solution(mesh):
    fine = Mesh(mesh.devices.reshape(2, 8, 4, 2, 4, 2), REP + FSDP)
    return jax.shard_map(
        per_device,
        mesh=fine,
        in_specs=(
            P(REP, FSDP),
            P(REP, FSDP),
            P(REP, None, FSDP),
            P(REP + FSDP, None),
            P(REP, FSDP),
            P(REP, FSDP),
        ),
        out_specs=(P(REP + FSDP, None), P(REP, FSDP), P(REP, FSDP), P(REP, FSDP)),
        check_vma=False,
    )
```

```python
import functools

import jax
import jax.numpy as jnp
from jax import lax
from jax.experimental import pallas as pl
from jax.experimental.pallas import tpu as pltpu
from jax.sharding import Mesh, PartitionSpec as P

D = 4608
N_REP = 128
FEAT = 576

rms_eps = 1e-06
inner_rate = 0.3
outer_rate = 0.7
outer_beta = 0.9

FSDP = ("x", "yh")
REP = ("yl", "z", "core")
SWAP = [(0, 1), (1, 0)]
f32 = jnp.float32
bf16 = jnp.bfloat16
S = jax.ShapeDtypeStruct
PARAMS = pltpu.CompilerParams(vmem_limit_bytes=24 * 2**20)


HBM = pl.BlockSpec(memory_space=pltpu.HBM)
CHEAP = pl.CostEstimate(flops=1000, bytes_accessed=1000, transcendentals=0)
ANY = pl.BlockSpec(memory_space=pl.ANY)
VMEM = pl.BlockSpec(memory_space=pltpu.VMEM)


def far(array):
    return pltpu.with_memory_space_constraint(array, pltpu.HBM)


ALONG_X = (2, 4, 6)
ACROSS = (1, 3, 5, 7)


def partner(bits):
    return [(i, i ^ bits) for i in range(8)]


def pack_kernel(cot_hbm, tok_hbm, out_ref, cot, tok, buffer, sems, in_sems):
    cot_copy = pltpu.make_async_copy(cot_hbm, cot, in_sems.at[0])
    tok_copy = pltpu.make_async_copy(tok_hbm, tok, in_sems.at[1])
    cot_copy.start()
    tok_copy.start()
    cot_copy.wait()
    buffer[0:1024] = cot[...].astype(f32).T.astype(bf16)
    tok_copy.wait()
    rows = []
    for j in range(8):
        part = tok[:, j * 128 : (j + 1) * 128].astype(f32)
        rows.append(jnp.sum(part * part, axis=0, keepdims=True))
    square = jnp.concatenate(rows, axis=0)
    high = square.astype(bf16).astype(f32)
    middle = (square - high).astype(bf16).astype(f32)
    low = square - high - middle
    tail = jnp.concatenate([high, middle, low, jnp.zeros_like(low)], axis=0).astype(bf16)
    buffer[1024:1056] = tail
    copies = []
    for peer in range(8):
        copies.append(pltpu.make_async_copy(buffer, out_ref.at[peer], sems.at[peer]))
        copies[-1].start()
    for copy in copies:
        copy.wait()


def weight_kernel(wt_ref, out_ref):
    out_ref[...] = wt_ref[...].astype(f32).T.astype(bf16)


def start_all(pairs, sems):
    copies = [pltpu.make_async_copy(src, dst, sems.at[i]) for i, (src, dst) in enumerate(pairs)]
    for copy in copies:
        copy.start()
    return copies


def grad_kernel(
    got_ref, tok_ref, w_ref, gain_ref,
    core_a_ref, core_b_ref, own_a_ref, own_b_ref, hid_hbm, gain_grad_ref,
    got, tok, weight, hid, total, sems,
):
    core = lax.axis_index("core")
    yl = lax.axis_index("yl")
    copies = start_all([(got_ref, got), (tok_ref, tok), (w_ref, weight)], sems)
    hid_copy = pltpu.make_async_copy(hid, hid_hbm, sems.at[3])
    gain_row = gain_ref[...].astype(f32)
    gain = jnp.broadcast_to(gain_row, (8, FEAT)).T[:, 0:1]
    copies[0].wait()
    square = jnp.zeros((8, 128), f32)
    for g in range(8):
        tail = got[g, 1024:1056].astype(f32)
        square += tail[0:8] + (tail[8:16] + tail[16:24])
    inv_rms = lax.rsqrt(square / D + rms_eps)
    copies[1].wait()
    for j in range(8):
        at = slice(j * 128, (j + 1) * 128)
        normed = tok[:, at].astype(f32) * inv_rms[j : j + 1]
        hid[:, at] = (normed * gain).astype(bf16)
    hid_copy.start()
    cot = jnp.concatenate([got[g, 0:1024] for g in range(8)], axis=1)
    grad = lax.dot_general(cot, hid[...], (((1,), (1,)), ((), ())), preferred_element_type=f32)
    copies[2].wait()
    w = weight[...].astype(f32)
    gain_grad_ref[...] = jnp.sum(w * grad, axis=0, keepdims=True) / gain_row
    total[...] = (w - inner_rate * grad).reshape(2, 32, 2, 8, FEAT)
    core_a_ref[...] = total[1 - yl, :, 1 - core].reshape(256, FEAT).astype(bf16)
    core_b_ref[...] = total[yl, :, 1 - core].reshape(256, FEAT).astype(bf16)
    own_a_ref[...] = total[1 - yl, :, core].reshape(256, FEAT)
    own_b_ref[...] = total[yl, :, core].reshape(256, FEAT)
    hid_copy.wait()


def pair_kernel(own, sibling, out):
    out[...] = (own[...] + sibling[...].astype(f32)).astype(bf16)


def three_kernel(own, sibling, arrived, after, out):
    out[...] = (own[...] + sibling[...].astype(f32) + arrived[...].astype(f32)).astype(bf16)


def keys_kernel(bits, hid_ref, wt_ref, after_ref, *outs):
    me = lax.axis_index("x") * 2 + lax.axis_index("yh")
    for bit, out in zip(bits, outs):
        group = me ^ bit
        hid = hid_ref[:, pl.ds(pl.multiple_of(group * 128, 128), 128)]
        out[...] = lax.dot_general(
            hid, wt_ref[...], (((0,), (0,)), ((), ())), preferred_element_type=f32
        ).astype(bf16)


def partial_keys(bits, hid, weight_t, after, name):
    return pl.pallas_call(
        functools.partial(keys_kernel, bits),
        out_shape=tuple(S((128, 1024), bf16) for _ in bits),
        in_specs=[VMEM, VMEM, ANY],
        compiler_params=PARAMS,
        name=name,
    )(hid, weight_t, after)


def per_device(tokens, norm_gain, key_weight, key_cotangent, global_fragment, outer_momentum):
    tok = tokens.T
    weight_t = key_weight[0].T
    packed = pl.pallas_call(
        pack_kernel,
        out_shape=pltpu.HBM((8, 1056, 128), bf16),
        in_specs=[HBM, HBM],
        out_specs=HBM,
        scratch_shapes=[
            pltpu.VMEM((128, 1024), bf16),
            pltpu.VMEM((FEAT, 1024), bf16),
            pltpu.VMEM((1056, 128), bf16),
            pltpu.SemaphoreType.DMA((8,)),
            pltpu.SemaphoreType.DMA((2,)),
        ],
        compiler_params=PARAMS,
        name="pack",
    )(far(key_cotangent), far(tok))
    got = lax.all_to_all(packed, FSDP, 0, 0)
    weight = pl.pallas_call(
        weight_kernel,
        out_shape=pltpu.HBM((1024, FEAT), bf16),
        out_specs=VMEM,
        compiler_params=PARAMS,
        cost_estimate=CHEAP,
        name="turn",
    )(weight_t)

    quarter = S((256, FEAT), bf16)
    core_a, core_b, own_a, own_b, hid, gain_grad = pl.pallas_call(
        grad_kernel,
        out_shape=(
            quarter, quarter, S((256, FEAT), f32), S((256, FEAT), f32),
            pltpu.HBM((FEAT, 1024), bf16), S((1, FEAT), f32),
        ),
        in_specs=[ANY, HBM, HBM, VMEM],
        out_specs=(VMEM, VMEM, VMEM, VMEM, HBM, VMEM),
        scratch_shapes=[
            pltpu.VMEM((8, 1056, 128), bf16),
            pltpu.VMEM((FEAT, 1024), bf16),
            pltpu.VMEM((1024, FEAT), bf16),
            pltpu.VMEM((FEAT, 1024), bf16),
            pltpu.VMEM((2, 32, 2, 8, FEAT), f32),
            pltpu.SemaphoreType.DMA((4,)),
        ],
        compiler_params=PARAMS,
        name="grad",
    )(got, far(tok), far(weight), norm_gain)

    sibling_a = lax.ppermute(core_a, "core", SWAP)
    sibling_b = lax.ppermute(core_b, "core", SWAP)
    pair = pl.pallas_call(pair_kernel, out_shape=quarter, compiler_params=PARAMS, name="pair")(own_a, sibling_a)
    arrived = lax.ppermute(pair, "yl", SWAP)
    along = partial_keys((0,) + ALONG_X, hid, weight_t, pair, "keys_along")
    pieces = [lax.ppermute(piece, FSDP, partner(bit)) for bit, piece in zip(ALONG_X, along[1:])]
    share = pl.pallas_call(
        three_kernel,
        out_shape=quarter,
        in_specs=[VMEM, VMEM, VMEM, ANY],
        compiler_params=PARAMS,
        name="share",
    )(own_b, sibling_b, arrived, pieces[0])
    z_parts = lax.all_to_all(share.reshape(32, 8, FEAT), "z", 0, 0)
    across = partial_keys(ACROSS, hid, weight_t, share, "keys_across")
    pieces += [lax.ppermute(piece, FSDP, partner(bit)) for bit, piece in zip(ACROSS, across)]
    summed = jnp.sum(z_parts.astype(f32), axis=0)

    avg_grad = global_fragment - summed / N_REP
    new_momentum = outer_beta * outer_momentum + avg_grad
    new_global = global_fragment - outer_rate * (avg_grad + outer_beta * new_momentum)
    key_out = along[0].astype(f32)
    for piece in pieces:
        key_out += piece.astype(f32)
    return (key_out.astype(bf16), gain_grad, new_global, new_momentum)


def solution(mesh):
    fine = Mesh(mesh.devices.reshape(2, 32, 2, 4, 2), REP + FSDP)
    return jax.shard_map(
        per_device,
        mesh=fine,
        in_specs=(
            P(REP, FSDP),
            P(REP, FSDP),
            P(REP, None, FSDP),
            P(REP + FSDP, None),
            P(REP, FSDP),
            P(REP, FSDP),
        ),
        out_specs=(P(REP + FSDP, None), P(REP, FSDP), P(REP, FSDP), P(REP, FSDP)),
        check_vma=False,
    )
```

```python
import jax
import jax.numpy as jnp
from jax import lax
from jax.experimental import pallas as pl
from jax.experimental.pallas import tpu as pltpu
from jax.sharding import Mesh, PartitionSpec as P

D = 4608
N_REP = 128
FEAT = 576

rms_eps = 1e-06
inner_rate = 0.3
outer_rate = 0.7
outer_beta = 0.9

ZC = ("z", "core")
FSDP = ("x", "yh")
REP = ("yl", "z", "core")
SWAP = [(0, 1), (1, 0)]
f32 = jnp.float32
bf16 = jnp.bfloat16
S = jax.ShapeDtypeStruct
PARAMS = pltpu.CompilerParams(vmem_limit_bytes=24 * 2**20)


HBM = pl.BlockSpec(memory_space=pltpu.HBM)
CHEAP = pl.CostEstimate(flops=1000, bytes_accessed=1000, transcendentals=0)
ANY = pl.BlockSpec(memory_space=pl.ANY)
VMEM = pl.BlockSpec(memory_space=pltpu.VMEM)


def far(array):
    return pltpu.with_memory_space_constraint(array, pltpu.HBM)


def ahead(first, second):
    pairs = []
    for z in range(32):
        for core, step in ((0, first), (1, second)):
            if step is not None:
                pairs.append((z * 2 + core, (z + (1 - 2 * core) * step) % 32 * 2 + core))
    return pairs


def pack_kernel(cot_hbm, tok_hbm, out_ref, cot, tok, buffer, sems, in_sems):
    cot_copy = pltpu.make_async_copy(cot_hbm, cot, in_sems.at[0])
    tok_copy = pltpu.make_async_copy(tok_hbm, tok, in_sems.at[1])
    cot_copy.start()
    tok_copy.start()
    cot_copy.wait()
    buffer[0:1024] = cot[...].astype(f32).T.astype(bf16)
    tok_copy.wait()
    rows = []
    for j in range(8):
        part = tok[:, j * 128 : (j + 1) * 128].astype(f32)
        rows.append(jnp.sum(part * part, axis=0, keepdims=True))
    square = jnp.concatenate(rows, axis=0)
    high = square.astype(bf16).astype(f32)
    middle = (square - high).astype(bf16).astype(f32)
    low = square - high - middle
    tail = jnp.concatenate([high, middle, low, jnp.zeros_like(low)], axis=0).astype(bf16)
    buffer[1024:1056] = tail
    copies = []
    for peer in range(8):
        copies.append(pltpu.make_async_copy(buffer, out_ref.at[peer], sems.at[peer]))
        copies[-1].start()
    for copy in copies:
        copy.wait()


def weight_kernel(wt_ref, out_ref):
    out_ref[...] = wt_ref[...].astype(f32).T.astype(bf16)


def start_all(pairs, sems):
    copies = [pltpu.make_async_copy(src, dst, sems.at[i]) for i, (src, dst) in enumerate(pairs)]
    for copy in copies:
        copy.start()
    return copies


def grad_kernel(
    got_ref, tok_ref, w_ref, gain_ref,
    core_a_ref, core_b_ref, own_a_ref, own_b_ref, hid_hbm, gain_grad_ref,
    got, tok, weight, hid, total, sems,
):
    core = lax.axis_index("core")
    yl = lax.axis_index("yl")
    copies = start_all([(got_ref, got), (tok_ref, tok), (w_ref, weight)], sems)
    hid_copy = pltpu.make_async_copy(hid, hid_hbm, sems.at[3])
    gain_row = gain_ref[...].astype(f32)
    gain = jnp.broadcast_to(gain_row, (8, FEAT)).T[:, 0:1]
    copies[0].wait()
    square = jnp.zeros((8, 128), f32)
    for g in range(8):
        tail = got[g, 1024:1056].astype(f32)
        square += tail[0:8] + (tail[8:16] + tail[16:24])
    inv_rms = lax.rsqrt(square / D + rms_eps)
    copies[1].wait()
    for j in range(8):
        at = slice(j * 128, (j + 1) * 128)
        normed = tok[:, at].astype(f32) * inv_rms[j : j + 1]
        hid[:, at] = (normed * gain).astype(bf16)
    hid_copy.start()
    cot = jnp.concatenate([got[g, 0:1024] for g in range(8)], axis=1)
    grad = lax.dot_general(cot, hid[...], (((1,), (1,)), ((), ())), preferred_element_type=f32)
    copies[2].wait()
    w = weight[...].astype(f32)
    gain_grad_ref[...] = jnp.sum(w * grad, axis=0, keepdims=True) / gain_row
    total[...] = (w - inner_rate * grad).reshape(2, 32, 16, FEAT)
    z = lax.axis_index("z")
    for t in range(16):
        own = (z + (1 - 2 * core) * t - core + 64) % 32
        sibling = (z + (2 * core - 1) * t - (1 - core) + 64) % 32
        core_a_ref[t] = total[1 - yl, sibling].astype(bf16)
        core_b_ref[t] = total[yl, sibling].astype(bf16)
        own_a_ref[t] = total[1 - yl, own]
        own_b_ref[t] = total[yl, own]
    hid_copy.wait()


def pair_kernel(own, sibling, out):
    out[...] = (own[...] + sibling[...].astype(f32)).astype(bf16)


def halve(total, keep, send):
    for i in range(total.shape[0] // 2):
        keep[i] = total[2 * i]
        send[i] = total[2 * i + 1].astype(bf16)


def share_kernel(own, sibling, arrived, keep, send):
    halve(own[...] + sibling[...].astype(f32) + arrived[...].astype(f32), keep, send)


def fold_kernel(kept, arrived, keep, send):
    halve(kept[...] + arrived[...].astype(f32), keep, send)


def end_kernel(kept, arrived, near_by, mine, other, total):
    core = lax.axis_index("core")
    held = kept[0] * (1 - core).astype(f32)
    both = held + arrived[0].astype(f32) + near_by[0].astype(f32)
    total[...] = both.reshape(2, 8, FEAT)
    mine[...] = total[core]
    other[...] = total[1 - core]


def fold(kept, arrived):
    n = kept.shape[0] // 2
    return pl.pallas_call(
        fold_kernel,
        out_shape=(S((n, 16, FEAT), f32), S((n, 16, FEAT), bf16)),
        compiler_params=PARAMS,
        name="fold",
    )(kept, arrived)


def keys_kernel(hid_ref, wt_ref, after_ref, out_ref):
    for group in range(8):
        hid = hid_ref[:, group * 128 : (group + 1) * 128]
        out_ref[group] = lax.dot_general(
            hid, wt_ref[...], (((0,), (0,)), ((), ())), preferred_element_type=f32
        ).astype(bf16)


def pass_kernel(array, after, out):
    pass


def per_device(tokens, norm_gain, key_weight, key_cotangent, global_fragment, outer_momentum):
    tok = tokens.T
    weight_t = key_weight[0].T
    packed = pl.pallas_call(
        pack_kernel,
        out_shape=pltpu.HBM((8, 1056, 128), bf16),
        in_specs=[HBM, HBM],
        out_specs=HBM,
        scratch_shapes=[
            pltpu.VMEM((128, 1024), bf16),
            pltpu.VMEM((FEAT, 1024), bf16),
            pltpu.VMEM((1056, 128), bf16),
            pltpu.SemaphoreType.DMA((8,)),
            pltpu.SemaphoreType.DMA((2,)),
        ],
        compiler_params=PARAMS,
        name="pack",
    )(far(key_cotangent), far(tok))
    got = lax.all_to_all(packed, FSDP, 0, 0)
    weight = pl.pallas_call(
        weight_kernel,
        out_shape=pltpu.HBM((1024, FEAT), bf16),
        out_specs=VMEM,
        compiler_params=PARAMS,
        cost_estimate=CHEAP,
        name="turn",
    )(weight_t)

    quarter = S((16, 16, FEAT), bf16)
    quarter_wide = S((16, 16, FEAT), f32)
    core_a, core_b, own_a, own_b, hid, gain_grad = pl.pallas_call(
        grad_kernel,
        out_shape=(
            quarter, quarter, quarter_wide, quarter_wide,
            pltpu.HBM((FEAT, 1024), bf16), S((1, FEAT), f32),
        ),
        in_specs=[ANY, HBM, HBM, VMEM],
        out_specs=(VMEM, VMEM, VMEM, VMEM, HBM, VMEM),
        scratch_shapes=[
            pltpu.VMEM((8, 1056, 128), bf16),
            pltpu.VMEM((FEAT, 1024), bf16),
            pltpu.VMEM((1024, FEAT), bf16),
            pltpu.VMEM((FEAT, 1024), bf16),
            pltpu.VMEM((2, 32, 16, FEAT), f32),
            pltpu.SemaphoreType.DMA((4,)),
        ],
        compiler_params=PARAMS,
        name="grad",
    )(got, far(tok), far(weight), norm_gain)

    sibling_a = lax.ppermute(core_a, "core", SWAP)
    sibling_b = lax.ppermute(core_b, "core", SWAP)
    pair = pl.pallas_call(pair_kernel, out_shape=quarter, compiler_params=PARAMS, name="pair")(own_a, sibling_a)
    arrived = lax.ppermute(pair, "yl", SWAP)
    keys = pl.pallas_call(
        keys_kernel,
        out_shape=pltpu.HBM((8, 128, 1024), bf16),
        in_specs=[VMEM, VMEM, ANY],
        out_specs=VMEM,
        compiler_params=PARAMS,
        name="keys",
    )(hid, weight_t, pair)

    keep, send = pl.pallas_call(
        share_kernel,
        out_shape=(S((8, 16, FEAT), f32), S((8, 16, FEAT), bf16)),
        compiler_params=PARAMS,
        name="share",
    )(own_b, sibling_b, arrived)
    keys = pl.pallas_call(
        pass_kernel,
        out_shape=pltpu.HBM((8, 128, 1024), bf16),
        in_specs=[HBM, ANY],
        out_specs=HBM,
        input_output_aliases={0: 0},
        compiler_params=PARAMS,
        name="pass_on",
    )(keys, send)
    key_parts = lax.all_to_all(keys, FSDP, 0, 0)
    for step in (1, 2, 4):
        keep, send = fold(keep, lax.ppermute(send, ZC, ahead(step, step)))
    near_by = lax.ppermute(keep.astype(bf16), ZC, ahead(None, 1))
    arrived = lax.ppermute(send, ZC, ahead(8, 9))
    mine, other = pl.pallas_call(
        end_kernel,
        out_shape=(S((8, FEAT), f32), S((8, FEAT), f32)),
        scratch_shapes=[pltpu.VMEM((2, 8, FEAT), f32)],
        compiler_params=PARAMS,
        name="end",
    )(keep, arrived, near_by)
    summed = mine + lax.ppermute(other, "core", SWAP)

    avg_grad = global_fragment - summed / N_REP
    new_momentum = outer_beta * outer_momentum + avg_grad
    new_global = global_fragment - outer_rate * (avg_grad + outer_beta * new_momentum)
    key_out = jnp.sum(key_parts.astype(f32), axis=0)
    return (key_out.astype(bf16), gain_grad, new_global, new_momentum)


def solution(mesh):
    fine = Mesh(mesh.devices.reshape(2, 32, 2, 4, 2), REP + FSDP)
    return jax.shard_map(
        per_device,
        mesh=fine,
        in_specs=(
            P(REP, FSDP),
            P(REP, FSDP),
            P(REP, None, FSDP),
            P(REP + FSDP, None),
            P(REP, FSDP),
            P(REP, FSDP),
        ),
        out_specs=(P(REP + FSDP, None), P(REP, FSDP), P(REP, FSDP), P(REP, FSDP)),
        check_vma=False,
    )
```

```python
import jax
import jax.numpy as jnp
from jax import lax
from jax.experimental import pallas as pl
from jax.experimental.pallas import tpu as pltpu
from jax.sharding import Mesh, PartitionSpec as P

D = 4608
N_REP = 128
FEAT = 576

rms_eps = 1e-06
inner_rate = 0.3
outer_rate = 0.7
outer_beta = 0.9

ZC = ("z", "core")
FSDP = ("x", "yh")
REP = ("yl", "z", "core")
SWAP = [(0, 1), (1, 0)]
f32 = jnp.float32
bf16 = jnp.bfloat16
S = jax.ShapeDtypeStruct
PARAMS = pltpu.CompilerParams(vmem_limit_bytes=24 * 2**20)


HBM = pl.BlockSpec(memory_space=pltpu.HBM)
LONG = 100 * 10**9
CHEAP = pl.CostEstimate(flops=1000, bytes_accessed=1000, transcendentals=0)
ANY = pl.BlockSpec(memory_space=pl.ANY)
VMEM = pl.BlockSpec(memory_space=pltpu.VMEM)


def far(array):
    return pltpu.with_memory_space_constraint(array, pltpu.HBM)


def ahead(first, second):
    pairs = []
    for z in range(32):
        for core, step in ((0, first), (1, second)):
            if step is not None:
                pairs.append((z * 2 + core, (z + (1 - 2 * core) * step) % 32 * 2 + core))
    return pairs


def pack_kernel(cot_hbm, tok_hbm, out_ref, cot, tok, buffer, last, sems, tail_sems, in_sems):
    cot_copy = pltpu.make_async_copy(cot_hbm, cot, in_sems.at[0])
    tok_copy = pltpu.make_async_copy(tok_hbm, tok, in_sems.at[1])
    cot_copy.start()
    tok_copy.start()
    cot_copy.wait()
    buffer[...] = cot[...].astype(f32).T.astype(bf16)
    copies = start_all([(buffer, out_ref.at[peer, pl.ds(0, 1024)]) for peer in range(8)], sems)
    tok_copy.wait()
    rows = []
    for j in range(8):
        part = tok[:, j * 128 : (j + 1) * 128].astype(f32)
        rows.append(jnp.sum(part * part, axis=0, keepdims=True))
    square = jnp.concatenate(rows, axis=0)
    high = square.astype(bf16).astype(f32)
    middle = (square - high).astype(bf16).astype(f32)
    low = square - high - middle
    tail = jnp.concatenate([high, middle, low, jnp.zeros_like(low)], axis=0).astype(bf16)
    last[...] = tail
    copies += start_all([(last, out_ref.at[peer, pl.ds(1024, 32)]) for peer in range(8)], tail_sems)
    for copy in copies:
        copy.wait()


def weight_kernel(wt_ref, out_ref):
    out_ref[...] = wt_ref[...].astype(f32).T.astype(bf16)


def start_all(pairs, sems):
    copies = [pltpu.make_async_copy(src, dst, sems.at[i]) for i, (src, dst) in enumerate(pairs)]
    for copy in copies:
        copy.start()
    return copies


def grad_kernel(
    got_ref, tok_ref, w_ref, gain_ref,
    core_a_ref, core_b_ref, own_a_ref, own_b_ref, hid_hbm, gain_grad_ref,
    got, tok, weight, hid, total, sems,
):
    core = lax.axis_index("core")
    yl = lax.axis_index("yl")
    copies = start_all([(got_ref, got), (tok_ref, tok), (w_ref, weight)], sems)
    hid_copy = pltpu.make_async_copy(hid, hid_hbm, sems.at[3])
    gain_row = gain_ref[...].astype(f32)
    gain = jnp.broadcast_to(gain_row, (8, FEAT)).T[:, 0:1]
    copies[0].wait()
    square = jnp.zeros((8, 128), f32)
    for g in range(8):
        tail = got[g, 1024:1056].astype(f32)
        square += tail[0:8] + (tail[8:16] + tail[16:24])
    inv_rms = lax.rsqrt(square / D + rms_eps)
    copies[1].wait()
    for j in range(8):
        at = slice(j * 128, (j + 1) * 128)
        normed = tok[:, at].astype(f32) * inv_rms[j : j + 1]
        hid[:, at] = (normed * gain).astype(bf16)
    hid_copy.start()
    cot = jnp.concatenate([got[g, 0:1024] for g in range(8)], axis=1)
    grad = lax.dot_general(cot, hid[...], (((1,), (1,)), ((), ())), preferred_element_type=f32)
    copies[2].wait()
    w = weight[...].astype(f32)
    gain_grad_ref[...] = jnp.sum(w * grad, axis=0, keepdims=True) / gain_row
    total[...] = (w - inner_rate * grad).reshape(2, 32, 16, FEAT)
    z = lax.axis_index("z")
    for t in range(16):
        own = (z + (1 - 2 * core) * t - core + 64) % 32
        sibling = (z + (2 * core - 1) * t - (1 - core) + 64) % 32
        core_a_ref[t] = total[1 - yl, sibling].astype(bf16)
        core_b_ref[t] = total[yl, sibling].astype(bf16)
        own_a_ref[t] = total[1 - yl, own]
        own_b_ref[t] = total[yl, own]
    hid_copy.wait()


def pair_kernel(own, sibling, out):
    out[...] = (own[...] + sibling[...].astype(f32)).astype(bf16)


def halve(total, keep, send):
    for i in range(total.shape[0] // 2):
        keep[i] = total[2 * i]
        send[i] = total[2 * i + 1].astype(bf16)


def share_kernel(own, sibling, arrived, after, keep, send):
    halve(own[...] + sibling[...].astype(f32) + arrived[...].astype(f32), keep, send)


def fold_kernel(kept, arrived, keep, send):
    halve(kept[...] + arrived[...].astype(f32), keep, send)


def end_kernel(kept, arrived, near_by, after, mine, other, total):
    core = lax.axis_index("core")
    held = kept[0] * (1 - core).astype(f32)
    both = held + arrived[0].astype(f32) + near_by[0].astype(f32)
    total[...] = both.reshape(2, 8, FEAT)
    mine[...] = total[core]
    other[...] = total[1 - core]


def fold(kept, arrived, flops):
    n = kept.shape[0] // 2
    return pl.pallas_call(
        fold_kernel,
        out_shape=(S((n, 16, FEAT), f32), S((n, 16, FEAT), bf16)),
        compiler_params=PARAMS,
        cost_estimate=pl.CostEstimate(flops=flops, bytes_accessed=1000, transcendentals=0),
        name="fold",
    )(kept, arrived)


def keys_kernel(hid_ref, wt_ref, after_ref, out_ref):
    for group in range(8):
        hid = hid_ref[:, group * 128 : (group + 1) * 128]
        out_ref[group] = lax.dot_general(
            hid, wt_ref[...], (((0,), (0,)), ((), ())), preferred_element_type=f32
        ).astype(bf16)


def pass_kernel(array, after, out):
    pass


def pass_on(array, after):
    return pl.pallas_call(
        pass_kernel,
        out_shape=pltpu.HBM(array.shape, array.dtype),
        in_specs=[HBM, ANY],
        out_specs=HBM,
        input_output_aliases={0: 0},
        compiler_params=PARAMS,
        name="pass_on",
    )(array, after)


def per_device(tokens, norm_gain, key_weight, key_cotangent, global_fragment, outer_momentum):
    tok = tokens.T
    weight_t = key_weight[0].T
    packed = pl.pallas_call(
        pack_kernel,
        out_shape=pltpu.HBM((8, 1056, 128), bf16),
        in_specs=[HBM, HBM],
        out_specs=HBM,
        scratch_shapes=[
            pltpu.VMEM((128, 1024), bf16),
            pltpu.VMEM((FEAT, 1024), bf16),
            pltpu.VMEM((1024, 128), bf16),
            pltpu.VMEM((32, 128), bf16),
            pltpu.SemaphoreType.DMA((8,)),
            pltpu.SemaphoreType.DMA((8,)),
            pltpu.SemaphoreType.DMA((2,)),
        ],
        compiler_params=PARAMS,
        name="pack",
    )(far(key_cotangent), far(tok))
    got = lax.all_to_all(packed, FSDP, 0, 0)
    weight = pl.pallas_call(
        weight_kernel,
        out_shape=pltpu.HBM((1024, FEAT), bf16),
        out_specs=VMEM,
        compiler_params=PARAMS,
        cost_estimate=CHEAP,
        name="turn",
    )(weight_t)

    quarter = S((16, 16, FEAT), bf16)
    quarter_wide = S((16, 16, FEAT), f32)
    core_a, core_b, own_a, own_b, hid, gain_grad = pl.pallas_call(
        grad_kernel,
        out_shape=(
            quarter, quarter, quarter_wide, quarter_wide,
            pltpu.HBM((FEAT, 1024), bf16), S((1, FEAT), f32),
        ),
        in_specs=[ANY, HBM, HBM, VMEM],
        out_specs=(VMEM, VMEM, VMEM, VMEM, HBM, VMEM),
        scratch_shapes=[
            pltpu.VMEM((8, 1056, 128), bf16),
            pltpu.VMEM((FEAT, 1024), bf16),
            pltpu.VMEM((1024, FEAT), bf16),
            pltpu.VMEM((FEAT, 1024), bf16),
            pltpu.VMEM((2, 32, 16, FEAT), f32),
            pltpu.SemaphoreType.DMA((4,)),
        ],
        compiler_params=PARAMS,
        name="grad",
    )(got, far(tok), far(weight), norm_gain)

    sibling_a = lax.ppermute(core_a, "core", SWAP)
    pair = pl.pallas_call(pair_kernel, out_shape=quarter, compiler_params=PARAMS, name="pair")(own_a, sibling_a)
    arrived = lax.ppermute(pair, "yl", SWAP)
    keys = pl.pallas_call(
        keys_kernel,
        out_shape=pltpu.HBM((8, 128, 1024), bf16),
        in_specs=[VMEM, VMEM, ANY],
        out_specs=VMEM,
        compiler_params=PARAMS,
        name="keys",
    )(hid, weight_t, pair)

    core_b = pl.pallas_call(
        pass_kernel,
        out_shape=quarter,
        in_specs=[ANY, HBM],
        out_specs=ANY,
        input_output_aliases={0: 0},
        compiler_params=PARAMS,
        name="hold",
    )(core_b, far(keys))
    sibling_b = lax.ppermute(core_b, "core", SWAP)
    keep, send = pl.pallas_call(
        share_kernel,
        out_shape=(S((8, 16, FEAT), f32), S((8, 16, FEAT), bf16)),
        in_specs=[VMEM, VMEM, VMEM, HBM],
        compiler_params=PARAMS,
        name="share",
    )(own_b, sibling_b, arrived, far(keys))
    keys = pass_on(keys, send)
    key_parts = lax.all_to_all(keys, FSDP, 0, 0)
    key_out = jnp.sum(key_parts.astype(f32), axis=0).astype(bf16)
    for step, flops in ((1, LONG), (2, 1000), (4, 1000)):
        keep, send = fold(keep, lax.ppermute(send, ZC, ahead(step, step)), flops)
    near_by = lax.ppermute(keep.astype(bf16), ZC, ahead(None, 1))
    arrived = lax.ppermute(send, ZC, ahead(8, 9))
    mine, other = pl.pallas_call(
        end_kernel,
        out_shape=(S((8, FEAT), f32), S((8, FEAT), f32)),
        in_specs=[VMEM, VMEM, VMEM, HBM],
        scratch_shapes=[pltpu.VMEM((2, 8, FEAT), f32)],
        compiler_params=PARAMS,
        name="end",
    )(keep, arrived, near_by, far(key_out))
    summed = mine + lax.ppermute(other, "core", SWAP)

    avg_grad = global_fragment - summed / N_REP
    new_momentum = outer_beta * outer_momentum + avg_grad
    new_global = global_fragment - outer_rate * (avg_grad + outer_beta * new_momentum)
    return (key_out, gain_grad, new_global, new_momentum)


def solution(mesh):
    fine = Mesh(mesh.devices.reshape(2, 32, 2, 4, 2), REP + FSDP)
    return jax.shard_map(
        per_device,
        mesh=fine,
        in_specs=(
            P(REP, FSDP),
            P(REP, FSDP),
            P(REP, None, FSDP),
            P(REP + FSDP, None),
            P(REP, FSDP),
            P(REP, FSDP),
        ),
        out_specs=(P(REP + FSDP, None), P(REP, FSDP), P(REP, FSDP), P(REP, FSDP)),
        check_vma=False,
    )
```

```python
import jax
import jax.numpy as jnp
from jax import lax
from jax.experimental import pallas as pl
from jax.experimental.pallas import tpu as pltpu
from jax.sharding import Mesh, PartitionSpec as P

D = 4608
N_REP = 128
FEAT = 576

rms_eps = 1e-06
inner_rate = 0.3
outer_rate = 0.7
outer_beta = 0.9

ZC = ("z", "core")
FSDP = ("x", "yh")
REP = ("yl", "z", "core")
SWAP = [(0, 1), (1, 0)]
f32 = jnp.float32
bf16 = jnp.bfloat16
S = jax.ShapeDtypeStruct
PARAMS = pltpu.CompilerParams(vmem_limit_bytes=24 * 2**20)


HBM = pl.BlockSpec(memory_space=pltpu.HBM)
LONG = 100 * 10**9
CHEAP = pl.CostEstimate(flops=1000, bytes_accessed=1000, transcendentals=0)
ANY = pl.BlockSpec(memory_space=pl.ANY)
VMEM = pl.BlockSpec(memory_space=pltpu.VMEM)


def far(array):
    return pltpu.with_memory_space_constraint(array, pltpu.HBM)


def ahead(first, second):
    pairs = []
    for z in range(32):
        for core, step in ((0, first), (1, second)):
            if step is not None:
                pairs.append((z * 2 + core, (z + (1 - 2 * core) * step) % 32 * 2 + core))
    return pairs


def pack_kernel(cot_hbm, tok_hbm, out_ref, cot, tok, buffer, last, sems, tail_sems, in_sems):
    cot_copy = pltpu.make_async_copy(cot_hbm, cot, in_sems.at[0])
    tok_copy = pltpu.make_async_copy(tok_hbm, tok, in_sems.at[1])
    cot_copy.start()
    tok_copy.start()
    cot_copy.wait()
    buffer[...] = cot[...].astype(f32).T.astype(bf16)
    copies = start_all([(buffer, out_ref.at[peer, pl.ds(0, 1024)]) for peer in range(8)], sems)
    tok_copy.wait()
    rows = []
    for j in range(8):
        part = tok[:, j * 128 : (j + 1) * 128].astype(f32)
        rows.append(jnp.sum(part * part, axis=0, keepdims=True))
    square = jnp.concatenate(rows, axis=0)
    high = square.astype(bf16).astype(f32)
    middle = (square - high).astype(bf16).astype(f32)
    low = square - high - middle
    tail = jnp.concatenate([high, middle, low, jnp.zeros_like(low)], axis=0).astype(bf16)
    last[...] = tail
    copies += start_all([(last, out_ref.at[peer, pl.ds(1024, 32)]) for peer in range(8)], tail_sems)
    for copy in copies:
        copy.wait()


def weight_kernel(wt_ref, out_ref):
    out_ref[...] = wt_ref[...].astype(f32).T.astype(bf16)


def start_all(pairs, sems):
    copies = [pltpu.make_async_copy(src, dst, sems.at[i]) for i, (src, dst) in enumerate(pairs)]
    for copy in copies:
        copy.start()
    return copies


def grad_kernel(
    got, tok_ref, w_ref, gain_ref,
    core_a_ref, core_b_ref, own_a_ref, own_b_ref, hid_hbm, gain_grad_ref,
    tok, weight, hid, total, sems,
):
    core = lax.axis_index("core")
    yl = lax.axis_index("yl")
    copies = start_all([(tok_ref, tok), (w_ref, weight)], sems)
    hid_copy = pltpu.make_async_copy(hid, hid_hbm, sems.at[2])
    gain_row = gain_ref[...].astype(f32)
    gain = jnp.broadcast_to(gain_row, (8, FEAT)).T[:, 0:1]
    square = jnp.zeros((8, 128), f32)
    for g in range(8):
        tail = got[g, 1024:1056].astype(f32)
        square += tail[0:8] + (tail[8:16] + tail[16:24])
    inv_rms = lax.rsqrt(square / D + rms_eps)
    copies[0].wait()
    for j in range(8):
        at = slice(j * 128, (j + 1) * 128)
        normed = tok[:, at].astype(f32) * inv_rms[j : j + 1]
        hid[:, at] = (normed * gain).astype(bf16)
    hid_copy.start()
    copies[1].wait()
    gain_sum = jnp.zeros((1, FEAT), f32)
    for m in range(4):
        rows = slice(256 * m, 256 * (m + 1))
        cot = jnp.concatenate([got[g, rows] for g in range(8)], axis=1)
        grad = lax.dot_general(cot, hid[...], (((1,), (1,)), ((), ())), preferred_element_type=f32)
        w = weight[rows].astype(f32)
        gain_sum += jnp.sum(w * grad, axis=0, keepdims=True)
        half = slice(m % 2 * 16, m % 2 * 16 + 16)
        total[m // 2, half] = (w - inner_rate * grad).reshape(16, 16, FEAT)
    gain_grad_ref[...] = gain_sum / gain_row
    z = lax.axis_index("z")
    for t in range(16):
        own = (z + (1 - 2 * core) * t - core + 64) % 32
        sibling = (z + (2 * core - 1) * t - (1 - core) + 64) % 32
        core_a_ref[t] = total[1 - yl, sibling].astype(bf16)
        core_b_ref[t] = total[yl, sibling].astype(bf16)
        own_a_ref[t] = total[1 - yl, own]
        own_b_ref[t] = total[yl, own]
    hid_copy.wait()


def pair_kernel(own, sibling, out):
    out[...] = (own[...] + sibling[...].astype(f32)).astype(bf16)


def halve(total, keep, send):
    for i in range(total.shape[0] // 2):
        keep[i] = total[2 * i]
        send[i] = total[2 * i + 1].astype(bf16)


def share_kernel(own, sibling, arrived, after, keep, send):
    halve(own[...] + sibling[...].astype(f32) + arrived[...].astype(f32), keep, send)


def fold_kernel(kept, arrived, keep, send):
    halve(kept[...] + arrived[...].astype(f32), keep, send)


def end_kernel(kept, arrived, near_by, after, mine, other, total):
    core = lax.axis_index("core")
    held = kept[0] * (1 - core).astype(f32)
    both = held + arrived[0].astype(f32) + near_by[0].astype(f32)
    total[...] = both.reshape(2, 8, FEAT)
    mine[...] = total[core]
    other[...] = total[1 - core]


def fold(kept, arrived, flops):
    n = kept.shape[0] // 2
    return pl.pallas_call(
        fold_kernel,
        out_shape=(S((n, 16, FEAT), f32), S((n, 16, FEAT), bf16)),
        compiler_params=PARAMS,
        cost_estimate=pl.CostEstimate(flops=flops, bytes_accessed=1000, transcendentals=0),
        name="fold",
    )(kept, arrived)


def keys_kernel(hid_ref, wt_ref, after_ref, out_ref):
    for group in range(8):
        hid = hid_ref[:, group * 128 : (group + 1) * 128]
        out_ref[group] = lax.dot_general(
            hid, wt_ref[...], (((0,), (0,)), ((), ())), preferred_element_type=f32
        ).astype(bf16)


def pass_kernel(array, after, out):
    pass


def pass_on(array, after):
    return pl.pallas_call(
        pass_kernel,
        out_shape=pltpu.HBM(array.shape, array.dtype),
        in_specs=[HBM, ANY],
        out_specs=HBM,
        input_output_aliases={0: 0},
        compiler_params=PARAMS,
        name="pass_on",
    )(array, after)


def per_device(tokens, norm_gain, key_weight, key_cotangent, global_fragment, outer_momentum):
    tok = tokens.T
    weight_t = key_weight[0].T
    packed = pl.pallas_call(
        pack_kernel,
        out_shape=pltpu.HBM((8, 1056, 128), bf16),
        in_specs=[HBM, HBM],
        out_specs=HBM,
        scratch_shapes=[
            pltpu.VMEM((128, 1024), bf16),
            pltpu.VMEM((FEAT, 1024), bf16),
            pltpu.VMEM((1024, 128), bf16),
            pltpu.VMEM((32, 128), bf16),
            pltpu.SemaphoreType.DMA((8,)),
            pltpu.SemaphoreType.DMA((8,)),
            pltpu.SemaphoreType.DMA((2,)),
        ],
        compiler_params=PARAMS,
        name="pack",
    )(far(key_cotangent), far(tok))
    got = lax.all_to_all(packed, FSDP, 0, 0)
    weight = pl.pallas_call(
        weight_kernel,
        out_shape=pltpu.HBM((1024, FEAT), bf16),
        out_specs=VMEM,
        compiler_params=PARAMS,
        cost_estimate=CHEAP,
        name="turn",
    )(weight_t)

    quarter = S((16, 16, FEAT), bf16)
    quarter_wide = S((16, 16, FEAT), f32)
    core_a, core_b, own_a, own_b, hid, gain_grad = pl.pallas_call(
        grad_kernel,
        out_shape=(
            quarter, quarter, quarter_wide, quarter_wide,
            pltpu.HBM((FEAT, 1024), bf16), S((1, FEAT), f32),
        ),
        in_specs=[VMEM, HBM, HBM, VMEM],
        out_specs=(VMEM, VMEM, VMEM, VMEM, HBM, VMEM),
        scratch_shapes=[
            pltpu.VMEM((FEAT, 1024), bf16),
            pltpu.VMEM((1024, FEAT), bf16),
            pltpu.VMEM((FEAT, 1024), bf16),
            pltpu.VMEM((2, 32, 16, FEAT), f32),
            pltpu.SemaphoreType.DMA((3,)),
        ],
        compiler_params=PARAMS,
        name="grad",
    )(got, far(tok), far(weight), norm_gain)

    sibling_a = lax.ppermute(core_a, "core", SWAP)
    pair = pl.pallas_call(pair_kernel, out_shape=quarter, compiler_params=PARAMS, name="pair")(own_a, sibling_a)
    arrived = lax.ppermute(pair, "yl", SWAP)
    keys = pl.pallas_call(
        keys_kernel,
        out_shape=pltpu.HBM((8, 128, 1024), bf16),
        in_specs=[VMEM, VMEM, ANY],
        out_specs=VMEM,
        compiler_params=PARAMS,
        name="keys",
    )(hid, weight_t, pair)

    core_b = pl.pallas_call(
        pass_kernel,
        out_shape=quarter,
        in_specs=[ANY, HBM],
        out_specs=ANY,
        input_output_aliases={0: 0},
        compiler_params=PARAMS,
        name="hold",
    )(core_b, far(keys))
    sibling_b = lax.ppermute(core_b, "core", SWAP)
    keep, send = pl.pallas_call(
        share_kernel,
        out_shape=(S((8, 16, FEAT), f32), S((8, 16, FEAT), bf16)),
        in_specs=[VMEM, VMEM, VMEM, HBM],
        compiler_params=PARAMS,
        name="share",
    )(own_b, sibling_b, arrived, far(keys))
    keys = pass_on(keys, send)
    key_parts = lax.all_to_all(keys, FSDP, 0, 0)
    key_out = jnp.sum(key_parts.astype(f32), axis=0).astype(bf16)
    for step, flops in ((1, LONG), (2, 1000), (4, 1000)):
        keep, send = fold(keep, lax.ppermute(send, ZC, ahead(step, step)), flops)
    near_by = lax.ppermute(keep.astype(bf16), ZC, ahead(None, 1))
    arrived = lax.ppermute(send, ZC, ahead(8, 9))
    mine, other = pl.pallas_call(
        end_kernel,
        out_shape=(S((8, FEAT), f32), S((8, FEAT), f32)),
        in_specs=[VMEM, VMEM, VMEM, HBM],
        scratch_shapes=[pltpu.VMEM((2, 8, FEAT), f32)],
        compiler_params=PARAMS,
        name="end",
    )(keep, arrived, near_by, far(key_out))
    summed = mine + lax.ppermute(other, "core", SWAP)

    avg_grad = global_fragment - summed / N_REP
    new_momentum = outer_beta * outer_momentum + avg_grad
    new_global = global_fragment - outer_rate * (avg_grad + outer_beta * new_momentum)
    return (key_out, gain_grad, new_global, new_momentum)


def solution(mesh):
    fine = Mesh(mesh.devices.reshape(2, 32, 2, 4, 2), REP + FSDP)
    return jax.shard_map(
        per_device,
        mesh=fine,
        in_specs=(
            P(REP, FSDP),
            P(REP, FSDP),
            P(REP, None, FSDP),
            P(REP + FSDP, None),
            P(REP, FSDP),
            P(REP, FSDP),
        ),
        out_specs=(P(REP + FSDP, None), P(REP, FSDP), P(REP, FSDP), P(REP, FSDP)),
        check_vma=False,
    )
```

```python
import jax
import jax.numpy as jnp
from jax import lax
from jax.experimental import pallas as pl
from jax.experimental.pallas import tpu as pltpu
from jax.sharding import Mesh, PartitionSpec as P

D = 4608
N_REP = 128
FEAT = 576

rms_eps = 1e-06
inner_rate = 0.3
outer_rate = 0.7
outer_beta = 0.9

ZC = ("z", "core")
FSDP = ("x", "yh")
REP = ("yl", "z", "core")
SWAP = [(0, 1), (1, 0)]
f32 = jnp.float32
bf16 = jnp.bfloat16
S = jax.ShapeDtypeStruct
PARAMS = pltpu.CompilerParams(vmem_limit_bytes=24 * 2**20)


HBM = pl.BlockSpec(memory_space=pltpu.HBM)
LONG = 100 * 10**9
CHEAP = pl.CostEstimate(flops=1000, bytes_accessed=1000, transcendentals=0)
ANY = pl.BlockSpec(memory_space=pl.ANY)
VMEM = pl.BlockSpec(memory_space=pltpu.VMEM)


def far(array):
    return pltpu.with_memory_space_constraint(array, pltpu.HBM)


def ahead(first, second):
    pairs = []
    for z in range(32):
        for core, step in ((0, first), (1, second)):
            if step is not None:
                pairs.append((z * 2 + core, (z + (1 - 2 * core) * step) % 32 * 2 + core))
    return pairs


def pack_kernel(cot_hbm, tok_hbm, out_ref, cot, tok, buffer, last, sems, tail_sems, in_sems):
    cot_copy = pltpu.make_async_copy(cot_hbm, cot, in_sems.at[0])
    tok_copy = pltpu.make_async_copy(tok_hbm, tok, in_sems.at[1])
    cot_copy.start()
    tok_copy.start()
    cot_copy.wait()
    buffer[...] = cot[...].astype(f32).T.astype(bf16)
    copies = start_all([(buffer, out_ref.at[peer, pl.ds(0, 1024)]) for peer in range(8)], sems)
    tok_copy.wait()
    rows = []
    for j in range(8):
        part = tok[:, j * 128 : (j + 1) * 128].astype(f32)
        rows.append(jnp.sum(part * part, axis=0, keepdims=True))
    square = jnp.concatenate(rows, axis=0)
    high = square.astype(bf16).astype(f32)
    middle = (square - high).astype(bf16).astype(f32)
    low = square - high - middle
    tail = jnp.concatenate([high, middle, low, jnp.zeros_like(low)], axis=0).astype(bf16)
    last[...] = tail
    copies += start_all([(last, out_ref.at[peer, pl.ds(1024, 32)]) for peer in range(8)], tail_sems)
    for copy in copies:
        copy.wait()


def weight_kernel(wt_ref, out_ref):
    out_ref[...] = wt_ref[...].astype(f32).T.astype(bf16)


def start_all(pairs, sems):
    copies = [pltpu.make_async_copy(src, dst, sems.at[i]) for i, (src, dst) in enumerate(pairs)]
    for copy in copies:
        copy.start()
    return copies


def grad_kernel(
    got, tok_ref, w_ref, gain_ref,
    core_a_ref, core_b_ref, own_a_ref, own_b_ref, hid_hbm, gain_grad_ref,
    tok, weight, hid, total, sems,
):
    core = lax.axis_index("core")
    yl = lax.axis_index("yl")
    copies = start_all([(tok_ref, tok), (w_ref, weight)], sems)
    hid_copy = pltpu.make_async_copy(hid, hid_hbm, sems.at[2])
    gain_row = gain_ref[...].astype(f32)
    gain = jnp.broadcast_to(gain_row, (8, FEAT)).T[:, 0:1]
    square = jnp.zeros((8, 128), f32)
    for g in range(8):
        tail = got[g, 1024:1056].astype(f32)
        square += tail[0:8] + (tail[8:16] + tail[16:24])
    inv_rms = lax.rsqrt(square / D + rms_eps)
    copies[0].wait()
    for j in range(8):
        at = slice(j * 128, (j + 1) * 128)
        normed = tok[:, at].astype(f32) * inv_rms[j : j + 1]
        hid[:, at] = (normed * gain).astype(bf16)
    hid_copy.start()
    gain_sum = jnp.zeros((1, FEAT), f32)
    for m in range(4):
        rows = slice(256 * m, 256 * (m + 1))
        cot = jnp.concatenate([got[g, rows] for g in range(8)], axis=1)
        grad = lax.dot_general(cot, hid[...], (((1,), (1,)), ((), ())), preferred_element_type=f32)
        if m == 0:
            copies[1].wait()
        w = weight[rows].astype(f32)
        gain_sum += jnp.sum(w * grad, axis=0, keepdims=True)
        half = slice(m % 2 * 16, m % 2 * 16 + 16)
        total[m // 2, half] = (w - inner_rate * grad).reshape(16, 16, FEAT)
    gain_grad_ref[...] = gain_sum / gain_row
    z = lax.axis_index("z")
    for t in range(16):
        own = (z + (1 - 2 * core) * t - core + 64) % 32
        sibling = (z + (2 * core - 1) * t - (1 - core) + 64) % 32
        core_a_ref[t] = total[1 - yl, sibling].astype(bf16)
        core_b_ref[t] = total[yl, sibling].astype(bf16)
        own_a_ref[t] = total[1 - yl, own]
        own_b_ref[t] = total[yl, own]
    hid_copy.wait()


def pair_kernel(own, sibling, out):
    out[...] = (own[...] + sibling[...].astype(f32)).astype(bf16)


def halve(total, keep, send):
    for i in range(total.shape[0] // 2):
        keep[i] = total[2 * i]
        send[i] = total[2 * i + 1].astype(bf16)


def share_kernel(own, sibling, arrived, after, keep, send):
    halve(own[...] + sibling[...].astype(f32) + arrived[...].astype(f32), keep, send)


def fold_kernel(kept, arrived, keep, send):
    halve(kept[...] + arrived[...].astype(f32), keep, send)


def end_kernel(kept, arrived, near_by, after, mine, other, total):
    core = lax.axis_index("core")
    held = kept[0] * (1 - core).astype(f32)
    both = held + arrived[0].astype(f32) + near_by[0].astype(f32)
    total[...] = both.reshape(2, 8, FEAT)
    mine[...] = total[core]
    other[...] = total[1 - core]


def fold(kept, arrived, flops):
    n = kept.shape[0] // 2
    return pl.pallas_call(
        fold_kernel,
        out_shape=(S((n, 16, FEAT), f32), S((n, 16, FEAT), bf16)),
        compiler_params=PARAMS,
        cost_estimate=pl.CostEstimate(flops=flops, bytes_accessed=1000, transcendentals=0),
        name="fold",
    )(kept, arrived)


def keys_kernel(hid_ref, wt_ref, after_ref, out_ref):
    for group in range(8):
        hid = hid_ref[:, group * 128 : (group + 1) * 128]
        out_ref[group] = lax.dot_general(
            hid, wt_ref[...], (((0,), (0,)), ((), ())), preferred_element_type=f32
        ).astype(bf16)


def pass_kernel(array, after, out):
    pass


def pass_on(array, after):
    return pl.pallas_call(
        pass_kernel,
        out_shape=pltpu.HBM(array.shape, array.dtype),
        in_specs=[HBM, ANY],
        out_specs=HBM,
        input_output_aliases={0: 0},
        compiler_params=PARAMS,
        name="pass_on",
    )(array, after)


def per_device(tokens, norm_gain, key_weight, key_cotangent, global_fragment, outer_momentum):
    tok = tokens.T
    weight_t = key_weight[0].T
    packed = pl.pallas_call(
        pack_kernel,
        out_shape=pltpu.HBM((8, 1056, 128), bf16),
        in_specs=[HBM, HBM],
        out_specs=HBM,
        scratch_shapes=[
            pltpu.VMEM((128, 1024), bf16),
            pltpu.VMEM((FEAT, 1024), bf16),
            pltpu.VMEM((1024, 128), bf16),
            pltpu.VMEM((32, 128), bf16),
            pltpu.SemaphoreType.DMA((8,)),
            pltpu.SemaphoreType.DMA((8,)),
            pltpu.SemaphoreType.DMA((2,)),
        ],
        compiler_params=PARAMS,
        name="pack",
    )(far(key_cotangent), far(tok))
    got = lax.all_to_all(packed, FSDP, 0, 0)
    weight = pl.pallas_call(
        weight_kernel,
        out_shape=pltpu.HBM((1024, FEAT), bf16),
        out_specs=VMEM,
        compiler_params=PARAMS,
        cost_estimate=CHEAP,
        name="turn",
    )(weight_t)

    quarter = S((16, 16, FEAT), bf16)
    quarter_wide = S((16, 16, FEAT), f32)
    core_a, core_b, own_a, own_b, hid, gain_grad = pl.pallas_call(
        grad_kernel,
        out_shape=(
            quarter, quarter, quarter_wide, quarter_wide,
            pltpu.HBM((FEAT, 1024), bf16), S((1, FEAT), f32),
        ),
        in_specs=[VMEM, HBM, HBM, VMEM],
        out_specs=(VMEM, VMEM, VMEM, VMEM, HBM, VMEM),
        scratch_shapes=[
            pltpu.VMEM((FEAT, 1024), bf16),
            pltpu.VMEM((1024, FEAT), bf16),
            pltpu.VMEM((FEAT, 1024), bf16),
            pltpu.VMEM((2, 32, 16, FEAT), f32),
            pltpu.SemaphoreType.DMA((3,)),
        ],
        compiler_params=PARAMS,
        name="grad",
    )(got, far(tok), far(weight), norm_gain)

    sibling_a = lax.ppermute(core_a, "core", SWAP)
    pair = pl.pallas_call(pair_kernel, out_shape=quarter, compiler_params=PARAMS, name="pair")(own_a, sibling_a)
    arrived = lax.ppermute(pair, "yl", SWAP)
    keys = pl.pallas_call(
        keys_kernel,
        out_shape=pltpu.HBM((8, 128, 1024), bf16),
        in_specs=[VMEM, VMEM, ANY],
        out_specs=VMEM,
        compiler_params=PARAMS,
        name="keys",
    )(hid, weight_t, pair)

    core_b = pl.pallas_call(
        pass_kernel,
        out_shape=quarter,
        in_specs=[ANY, HBM],
        out_specs=ANY,
        input_output_aliases={0: 0},
        compiler_params=PARAMS,
        name="hold",
    )(core_b, far(keys))
    sibling_b = lax.ppermute(core_b, "core", SWAP)
    keep, send = pl.pallas_call(
        share_kernel,
        out_shape=(S((8, 16, FEAT), f32), S((8, 16, FEAT), bf16)),
        in_specs=[VMEM, VMEM, VMEM, HBM],
        compiler_params=PARAMS,
        name="share",
    )(own_b, sibling_b, arrived, far(keys))
    keys = pass_on(keys, send)
    key_parts = lax.all_to_all(keys, FSDP, 0, 0)
    key_out = jnp.sum(key_parts.astype(f32), axis=0).astype(bf16)
    for step, flops in ((1, LONG), (2, 1000), (4, 1000)):
        keep, send = fold(keep, lax.ppermute(send, ZC, ahead(step, step)), flops)
    near_by = lax.ppermute(keep.astype(bf16), ZC, ahead(None, 1))
    arrived = lax.ppermute(send, ZC, ahead(8, 9))
    mine, other = pl.pallas_call(
        end_kernel,
        out_shape=(S((8, FEAT), f32), S((8, FEAT), f32)),
        in_specs=[VMEM, VMEM, VMEM, HBM],
        scratch_shapes=[pltpu.VMEM((2, 8, FEAT), f32)],
        compiler_params=PARAMS,
        name="end",
    )(keep, arrived, near_by, far(key_out))
    summed = mine + lax.ppermute(other, "core", SWAP)

    avg_grad = global_fragment - summed / N_REP
    new_momentum = outer_beta * outer_momentum + avg_grad
    new_global = global_fragment - outer_rate * (avg_grad + outer_beta * new_momentum)
    return (key_out, gain_grad, new_global, new_momentum)


def solution(mesh):
    fine = Mesh(mesh.devices.reshape(2, 32, 2, 4, 2), REP + FSDP)
    return jax.shard_map(
        per_device,
        mesh=fine,
        in_specs=(
            P(REP, FSDP),
            P(REP, FSDP),
            P(REP, None, FSDP),
            P(REP + FSDP, None),
            P(REP, FSDP),
            P(REP, FSDP),
        ),
        out_specs=(P(REP + FSDP, None), P(REP, FSDP), P(REP, FSDP), P(REP, FSDP)),
        check_vma=False,
    )
```
